512 devices in a mesh: seq: 32 (over x, y, core), batch: 16 (over z).
Axes of the slice: x: 4, y: 4, z: 16, core: 2. Of those that a mesh axis runs over, the one named last changes fastest.
Arguments:
- queries: bfloat16 [16, 16384, 256], P('batch', 'seq'), may hold values from -6 to 6
- key_rows: bfloat16 [16, 16384, 256], P('batch', 'seq'), may hold values from -6 to 6
- value_rows: bfloat16 [16, 16384, 256], P('batch', 'seq'), may hold values from -6 to 6
- step_rates: float32 [16, 16384], P('batch', 'seq'), may hold values from 0.02 to 0.2
- cotangent: bfloat16 [16, 16384, 256], P('batch', 'seq'), may hold values from -0.01171875 to 0.01171875
- fast_init: float32 [768, 256], P('batch'), may hold values from -0.375 to 0.375
Outputs:
- layer_out: bfloat16 [16, 16384, 256], P('batch', 'seq')
- init_grad: float32 [768, 256], P('batch')
The draws below stay inside these ranges and needn't reach their ends.
All inputs are finite; a program needn't handle non-finite values.
Results may differ from the reference program's by a relative error of at most 0.0012.
Values sent between devices are 32-bit elements; how exact they have to be, the bound alone decides.
A program may use at most 64 MiB of HBM per device.

```python
import math
import jax
import jax.numpy as jnp
from jax import lax

HD = 256
FH = 256
SEQ_LEN = 16384
SEQS = 16


def level_of(rng, shape, pieces, smallest, largest):
    level = 1.0
    for axis_at, shards_of in pieces:
        steps = jax.random.uniform(jax.random.fold_in(jax.random.fold_in(rng, 6), axis_at), (shards_of,), jnp.float32, smallest / len(pieces), largest / len(pieces))
        level = level * jnp.repeat(jnp.exp(steps), shape[axis_at] // shards_of).reshape((-1,) + (1,) * (len(shape) - 1 - axis_at))
    return level


def gaussian(key, dims, spread, bound, split=(), held_as=jnp.bfloat16):
    drawn = spread * jax.random.normal(key, dims, jnp.float32)
    if split:
        drawn = drawn * level_of(key, dims, split, -0.22, 0.18)
    return jnp.clip(drawn, -bound, bound).astype(held_as)


def setup_inputs(seed: int = 0) -> dict:
    streams_of = jax.random.split(jax.random.key(seed), 7)
    queries = gaussian(streams_of[0], (SEQS, SEQ_LEN, HD), 1.0, 6.0, ((0, 16), (1, 32)))
    key_rows = gaussian(streams_of[1], (SEQS, SEQ_LEN, HD), 1.0, 6.0, ((0, 16), (1, 32)))
    value_rows = gaussian(streams_of[2], (SEQS, SEQ_LEN, HD), 1.0, 6.0, ((0, 16), (1, 32)))
    step_rates = jnp.clip(jnp.exp(math.log(0.2) - 2.3025851 * jax.random.uniform(streams_of[3], (SEQS, SEQ_LEN), jnp.float32) ** level_of(streams_of[3], (SEQS, SEQ_LEN), ((0, 16), (1, 32)), -0.2, 0.2)), 0.02, 0.2)
    cotangent = gaussian(streams_of[4], (SEQS, SEQ_LEN, HD), ((SEQ_LEN * SEQS) ** -0.5), 0.01171875, ((0, 16), (1, 32)))
    fast_init = gaussian(streams_of[5], (3 * HD, FH), HD ** -0.5, 0.375, ((0, 16),), jnp.float32)
    return dict(queries=queries, key_rows=key_rows, value_rows=value_rows, step_rates=step_rates, cotangent=cotangent, fast_init=fast_init)


def swiglu_apply(weights, row_block):
    high = lax.Precision.HIGHEST
    projected = jnp.dot(row_block, weights[0], precision=high, preferred_element_type=jnp.float32)
    gate_pre = jnp.dot(row_block, weights[1], precision=high, preferred_element_type=jnp.float32)
    hidden = jax.nn.silu(gate_pre) * projected
    return jnp.dot(hidden, weights[2].T, precision=high, preferred_element_type=jnp.float32)

def inner_loss(weights, key_block, value_block, scaled):
    return -jnp.sum(scaled[:, None] * swiglu_apply(weights, key_block) * value_block)

def inner_grad(weights, key_block, value_block, scaled):
    return jax.grad(inner_loss)(weights, key_block, value_block, scaled)

def reference(queries, key_rows, value_rows, step_rates, cotangent, fast_init):
    initial = fast_init.reshape(3, HD, FH)
    divisor = math.sqrt(SEQ_LEN)

    def one_sequence(items):
        query_seq, key_seq, value_seq, rate_seq, cot_seq = items
        query_block = query_seq.astype(jnp.float32)
        key_block = key_seq.astype(jnp.float32)
        value_block = value_seq.astype(jnp.float32)
        scaled = rate_seq / divisor

        def forward(weights):
            middle = weights - inner_grad(weights, key_block, value_block, scaled)
            final = middle - inner_grad(middle, key_block, value_block, scaled)
            return swiglu_apply(final, query_block)
        result, pull_back = jax.vjp(forward, initial)
        grads = pull_back(cot_seq.astype(jnp.float32))[0]
        return (result.astype(jnp.bfloat16), grads)
    outputs, grads = lax.map(one_sequence, (queries, key_rows, value_rows, step_rates, cotangent))
    return (outputs, lax.optimization_barrier(jnp.sum(grads, axis=0)).reshape(3 * HD, FH))
```

```python
import math

import jax
import jax.numpy as jnp
from jax import lax
from jax.experimental import pallas as pl
from jax.experimental.pallas import tpu as pltpu
from jax.sharding import Mesh
from jax.sharding import PartitionSpec as P

MESH = pl.DeviceIdType.MESH
SEQ = ("x", "y", "c")
F32 = jnp.float32
BF16 = jnp.bfloat16
SIDE = 4
CHIPS = SIDE * SIDE
LAYERS = 16
TILE = 8
TOKENS = 512
WIDTH = 256
HALF = 128
GROUPS = 6
ROWS = 256
BOTH = 2 * TOKENS


def far_first():
    hops = lambda step: min(step, SIDE - step)
    steps = [(dx, dy) for dx in range(SIDE) for dy in range(SIDE) if dx or dy]
    return sorted(steps, key=lambda s: -(hops(s[0]) + hops(s[1])))


PEERS = far_first()
NPEERS = len(PEERS)
Z_STEPS = sorted(range(1, LAYERS), key=lambda dz: -min(dz, LAYERS - dz))


def split(value):
    high = value.astype(BF16)
    return high, (value - high.astype(F32)).astype(BF16)


def dot(a, b):
    return jnp.dot(a, b, preferred_element_type=F32)


def kernel(
    q_in, k_in, v_in, rates_in, cot_in, w_in,
    out_ref, grad_ref,
    tok, mine, theirs, tok_b, tok_t, rates_own, rates_other, eta, w_own,
    whole, part, parts, chunk, prev, fin,
    w_ab, w_lo, w_c,
    pre_p, pre_g, pre_u, c1, c2, c3, c4,
    d_hi, d_lo, e_pair, hid, w_ct, out_part, out_other, z_parts, z_sum, tail,
    load_sem, x_send, x_recv, r_send, r_recv, o_send, o_recv,
    rs_send, rs_recv, ag_send, ag_recv, z_send, z_recv, y_send, y_recv, t_send, t_recv, f_send, f_recv,
):
    x, y, c, z = (lax.axis_index(name) for name in ("x", "y", "c", "z"))
    me = x * SIDE + y
    other = (x, y, 1 - c, z)

    loads = [
        pltpu.make_async_copy(src.at[0], tok.at[i], load_sem.at[i])
        for i, src in enumerate((k_in, v_in, q_in, cot_in))
    ]
    loads.append(pltpu.make_async_copy(rates_in, rates_own, load_sem.at[4]))
    for load in loads:
        load.start()

    def peer(step):
        px = lax.rem(x + step[0], SIDE)
        py = lax.rem(y + step[1], SIDE)
        return (px, py, c, z), px * SIDE + py

    def z_peer(dz):
        return (x, y, c, lax.rem(z + dz, LAYERS))

    barrier = pltpu.get_barrier_semaphore()
    for dz in Z_STEPS:
        pl.semaphore_signal(barrier, inc=1, device_id=z_peer(dz), device_id_type=MESH)
    for step in PEERS:
        pl.semaphore_signal(barrier, inc=1, device_id=peer(step)[0], device_id_type=MESH)
    pl.semaphore_signal(barrier, inc=1, device_id=other, device_id_type=MESH)

    for half in range(2):
        @pl.when(c == half)
        def _():
            w_own[...] = w_in[:, half * HALF : (half + 1) * HALF].reshape(GROUPS, TILE, HALF)

    for load in loads:
        load.wait()
    for i in range(4):
        mine[i] = tok[i].astype(F32)
    divisor = math.sqrt(lax.axis_size(SEQ) * TOKENS)
    eta[0:TOKENS] = -jnp.broadcast_to(rates_own[...] / divisor, (HALF, TOKENS)).T

    pl.semaphore_wait(barrier, LAYERS - 1 + NPEERS + 1)

    sub = lax.rem(me + GROUPS * LAYERS - GROUPS * z, CHIPS)
    group = GROUPS * z + sub
    at = lax.div(group, CHIPS)

    def z_copy(dz):
        return pltpu.make_async_remote_copy(
            w_own.at[sub], chunk.at[at], z_send.at[dz - 1], z_recv.at[at],
            device_id=z_peer(dz), device_id_type=MESH,
        )

    @pl.when(sub < GROUPS)
    def _():
        for dz in Z_STEPS:
            z_copy(dz).start()
        chunk[pl.ds(at, 1)] = w_own[pl.ds(sub, 1)]

    swaps = [
        pltpu.make_async_remote_copy(
            mine.at[i], theirs.at[i], x_send.at[i], x_recv.at[i], device_id=other, device_id_type=MESH
        )
        for i in range(4)
    ]
    swaps.append(
        pltpu.make_async_remote_copy(
            rates_own, rates_other, r_send, r_recv, device_id=other, device_id_type=MESH
        )
    )
    for swap in swaps:
        swap.start()

    for i in range(4):
        tok_b[i, 0:TOKENS] = tok[i]
        tok_t[i, :, 0:TOKENS] = mine[i].T.astype(BF16)
    for swap in swaps:
        swap.wait()
    eta[TOKENS:BOTH] = -jnp.broadcast_to(rates_other[...] / divisor, (HALF, TOKENS)).T
    for i in range(4):
        tok_b[i, TOKENS:BOTH] = theirs[i].astype(BF16)
        tok_t[i, :, TOKENS:BOTH] = theirs[i].T.astype(BF16)

    for j in range(GROUPS):
        owner = lax.div(CHIPS * j + me, GROUPS)

        @pl.when(owner != z)
        def _():
            pltpu.make_async_remote_copy(
                w_own.at[0], chunk.at[j], z_send.at[0], z_recv.at[j], device_id=other, device_id_type=MESH
            ).wait_recv()

    @pl.when(sub < GROUPS)
    def _():
        for dz in Z_STEPS:
            z_copy(dz).wait_send()

    def gather(stage):
        copies = [
            pltpu.make_async_remote_copy(
                chunk, whole.at[stage, :, me], ag_send.at[k], ag_recv.at[k],
                device_id=peer(step)[0], device_id_type=MESH,
            )
            for k, step in enumerate(PEERS)
        ]
        for copy in copies:
            copy.start()
        whole[stage, :, pl.ds(me, 1)] = chunk[...].reshape(GROUPS, 1, TILE, HALF)
        return copies

    def scatter():
        copies = []
        for k, step in enumerate(PEERS):
            device, chip = peer(step)
            copies.append(
                pltpu.make_async_remote_copy(
                    part.at[:, chip], parts.at[k], rs_send.at[k], rs_recv.at[k],
                    device_id=device, device_id_type=MESH,
                )
            )
        for copy in copies:
            copy.start()
        return copies

    def reduced(copies):
        for copy in copies:
            copy.wait()
        total = part[:, pl.ds(me, 1)].reshape(GROUPS, TILE, HALF)
        for k in range(NPEERS):
            total = total + parts[k]
        return total

    def weights(stage):
        for i in range(2):
            high, low = split(whole[stage, 2 * i : 2 * i + 2].reshape(WIDTH, HALF))
            w_ab[:, i * HALF : (i + 1) * HALF] = high
            w_lo[:, i * HALF : (i + 1) * HALF] = low
        high, low = split(whole[stage, 4:6].reshape(WIDTH, HALF))
        w_c[:, 0:HALF] = high
        w_c[:, HALF:] = low

    def projected(first, second, rows):
        pg = dot(tok_b[first, rows], w_ab[...]) + dot(tok_b[first, rows], w_lo[...])
        uu = dot(tok_b[second, rows], w_c[...])
        return pg[:, :HALF], pg[:, HALF:], uu[:, :HALF] + uu[:, HALF:]

    def keep(rows, dp, dg, e):
        for i, value in enumerate((dp, dg)):
            high, low = split(value)
            d_hi[rows, i * HALF : (i + 1) * HALF] = high
            d_lo[rows, i * HALF : (i + 1) * HALF] = low
        high, low = split(e)
        e_pair[rows, 0:HALF] = high
        e_pair[rows, HALF:] = low

    def contract(first, second):
        ab = dot(tok_t[first], d_hi[...]) + dot(tok_t[first], d_lo[...])
        cc = dot(tok_t[second], e_pair[...])
        part[0:2] = ab[:, :HALF].reshape(2, CHIPS, TILE, HALF)
        part[2:4] = ab[:, HALF:].reshape(2, CHIPS, TILE, HALF)
        part[4:6] = (cc[:, :HALF] + cc[:, HALF:]).reshape(2, CHIPS, TILE, HALF)

    def token_loop(body):
        def step(i, carry):
            body(pl.ds(pl.multiple_of(i * ROWS, ROWS), ROWS))
            return carry

        lax.fori_loop(0, BOTH // ROWS, step, 0)

    def sigmoid(g):
        return 1.0 / (1.0 + jnp.exp(-g))

    def inner(stage):
        weights(stage)

        def body(rows):
            p, g, u = projected(0, 1, rows)
            s = sigmoid(g)
            act = g * s
            slope = s + act * (1.0 - s)
            rate = eta[rows]
            f1 = rate * act
            f3 = rate * p * slope
            pre_p[rows] = p
            pre_g[rows] = g
            pre_u[rows] = u
            c1[stage, rows] = f1
            c3[stage, rows] = f3
            keep(rows, f1 * u, f3 * u, f1 * p)

        token_loop(body)
        contract(0, 1)

    def inner_second(stage):
        def body(rows):
            p, g, u = pre_p[rows], pre_g[rows], pre_u[rows]
            s = sigmoid(g)
            slope = s + g * s * (1.0 - s)
            bend = s * (1.0 - s) * (2.0 + g * (1.0 - 2.0 * s))
            w = eta[rows] * u
            c2[stage, rows] = w * slope
            c4[stage, rows] = w * p * bend

        token_loop(body)

    def hessian(stage, direction):
        weights(direction)

        def body(rows):
            p, g, u = projected(0, 1, rows)
            f1, f2, f3, f4 = c1[stage, rows], c2[stage, rows], c3[stage, rows], c4[stage, rows]
            keep(rows, f1 * u + f2 * g, f3 * u + f2 * p + f4 * g, f3 * g + f1 * p)

        token_loop(body)
        contract(0, 1)

    prev[...] = chunk[...]
    gathers = gather(0)
    for copy in gathers:
        copy.wait()
    for stage in range(2):
        inner(stage)
        copies = scatter()
        inner_second(stage)
        chunk[...] = prev[...] - reduced(copies)
        prev[...] = chunk[...]
        gathers = gather(stage + 1)
        for copy in gathers:
            copy.wait()

    weights(2)
    w_ct[0:HALF] = w_c[:, 0:HALF].astype(F32).T.astype(BF16)
    w_ct[HALF:] = w_c[:, HALF:].astype(F32).T.astype(BF16)

    def outer(rows):
        p, g, u = projected(2, 3, rows)
        s = sigmoid(g)
        act = g * s
        slope = s + act * (1.0 - s)
        h = act * p
        keep(rows, u * act, u * p * slope, h)

    token_loop(outer)
    contract(2, 3)
    copies = scatter()

    def partial_out(rows):
        high = e_pair[rows, 0:HALF]
        low = e_pair[rows, HALF:]
        return dot(high, w_ct[0:HALF]) + (dot(high, w_ct[HALF:]) + dot(low, w_ct[0:HALF]))

    out_part[...] = partial_out(pl.ds(TOKENS, TOKENS))
    swap = pltpu.make_async_remote_copy(
        out_part, out_other, o_send, o_recv, device_id=other, device_id_type=MESH
    )
    swap.start()
    hid[...] = partial_out(pl.ds(0, TOKENS))
    chunk[...] = reduced(copies)
    prev[...] = chunk[...]
    gathers = gather(3)
    swap.wait()
    out_ref[0] = (hid[...] + out_other[...]).astype(BF16)
    for copy in gathers:
        copy.wait()

    hessian(1, 3)
    copies = scatter()
    chunk[...] = prev[...] - reduced(copies)
    prev[...] = chunk[...]
    gathers = gather(4)
    for copy in gathers:
        copy.wait()

    hessian(0, 4)
    copies = scatter()
    fin[...] = prev[...] - reduced(copies)

    def to_owner(j):
        target_group = CHIPS * j + me
        target = lax.div(target_group, GROUPS)
        slot = lax.rem(target + LAYERS - z, LAYERS)
        return target, pltpu.make_async_remote_copy(
            fin.at[j], z_parts.at[slot], y_send.at[j], y_recv.at[slot],
            device_id=(x, y, c, target), device_id_type=MESH,
        )

    for j in range(GROUPS):
        target, copy = to_owner(j)

        @pl.when(target != z)
        def _():
            copy.start()

    @pl.when(sub < GROUPS)
    def _():
        total = fin[pl.ds(at, 1)].reshape(TILE, HALF)
        for slot in range(1, LAYERS):
            pltpu.make_async_remote_copy(
                fin.at[0], z_parts.at[slot], y_send.at[0], y_recv.at[slot],
                device_id=other, device_id_type=MESH,
            ).wait_recv()
        for slot in range(1, LAYERS):
            total = total + z_parts[slot]
        z_sum[...] = total
        tail[pl.ds(c, 1), pl.ds(sub, 1)] = total.reshape(1, 1, TILE, HALF)
        for k, step in enumerate(PEERS):
            pltpu.make_async_remote_copy(
                z_sum, tail.at[c, sub], t_send.at[k], t_recv.at[sub],
                device_id=peer(step)[0], device_id_type=MESH,
            ).start()

    for j in range(GROUPS):
        target, copy = to_owner(j)

        @pl.when(target != z)
        def _():
            copy.wait_send()

    for s in range(GROUPS):
        source = lax.rem(GROUPS * z + s, CHIPS)

        @pl.when(source != me)
        def _():
            pltpu.make_async_remote_copy(
                z_sum, tail.at[c, s], t_send.at[0], t_recv.at[s], device_id=other, device_id_type=MESH
            ).wait_recv()

    swap = pltpu.make_async_remote_copy(
        tail.at[c], tail.at[c], f_send, f_recv, device_id=other, device_id_type=MESH
    )
    swap.start()

    @pl.when(sub < GROUPS)
    def _():
        for k, step in enumerate(PEERS):
            pltpu.make_async_remote_copy(
                z_sum, tail.at[c, sub], t_send.at[k], t_recv.at[sub],
                device_id=peer(step)[0], device_id_type=MESH,
            ).wait_send()

    swap.wait()
    for half in range(2):
        grad_ref[:, half * HALF : (half + 1) * HALF] = tail[half].reshape(GROUPS * TILE, HALF)


def body(queries, key_rows, value_rows, step_rates, cotangent, fast_init):
    vmem = lambda *shape: pltpu.VMEM(shape, F32)
    half = lambda *shape: pltpu.VMEM(shape, BF16)
    dma = lambda *shape: pltpu.SemaphoreType.DMA(shape)
    any_spec = pl.BlockSpec(memory_space=pl.ANY)
    vmem_spec = pl.BlockSpec(memory_space=pltpu.VMEM)
    return pl.pallas_call(
        kernel,
        out_shape=(
            jax.ShapeDtypeStruct(queries.shape, BF16),
            jax.ShapeDtypeStruct(fast_init.shape, F32),
        ),
        in_specs=[any_spec] * 5 + [vmem_spec],
        out_specs=(vmem_spec, vmem_spec),
        scratch_shapes=[
            half(4, TOKENS, WIDTH),
            vmem(4, TOKENS, WIDTH),
            vmem(4, TOKENS, WIDTH),
            half(4, BOTH, WIDTH),
            half(4, WIDTH, BOTH),
            vmem(1, TOKENS),
            vmem(1, TOKENS),
            vmem(BOTH, HALF),
            vmem(GROUPS, TILE, HALF),
            vmem(5, GROUPS, CHIPS, TILE, HALF),
            vmem(GROUPS, CHIPS, TILE, HALF),
            vmem(NPEERS, GROUPS, TILE, HALF),
            vmem(GROUPS, TILE, HALF),
            vmem(GROUPS, TILE, HALF),
            vmem(GROUPS, TILE, HALF),
            half(WIDTH, WIDTH),
            half(WIDTH, WIDTH),
            half(WIDTH, WIDTH),
            vmem(BOTH, HALF),
            vmem(BOTH, HALF),
            vmem(BOTH, HALF),
            vmem(2, BOTH, HALF),
            vmem(2, BOTH, HALF),
            vmem(2, BOTH, HALF),
            vmem(2, BOTH, HALF),
            half(BOTH, WIDTH),
            half(BOTH, WIDTH),
            half(BOTH, WIDTH),
            vmem(TOKENS, WIDTH),
            half(WIDTH, WIDTH),
            vmem(TOKENS, WIDTH),
            vmem(TOKENS, WIDTH),
            vmem(LAYERS, TILE, HALF),
            vmem(TILE, HALF),
            vmem(2, GROUPS, TILE, HALF),
            dma(5),
            dma(4), dma(4),
            pltpu.SemaphoreType.DMA, pltpu.SemaphoreType.DMA,
            pltpu.SemaphoreType.DMA, pltpu.SemaphoreType.DMA,
            dma(NPEERS), dma(NPEERS),
            dma(NPEERS), dma(NPEERS),
            dma(LAYERS), dma(GROUPS),
            dma(GROUPS), dma(LAYERS),
            dma(NPEERS), dma(GROUPS),
            pltpu.SemaphoreType.DMA, pltpu.SemaphoreType.DMA,
        ],
        compiler_params=pltpu.CompilerParams(
            collective_id=0, has_side_effects=True, vmem_limit_bytes=56 * 2**20
        ),
    )(queries, key_rows, value_rows, step_rates, cotangent, fast_init)


def solution(mesh):
    torus = Mesh(
        mesh.devices.reshape(SIDE, SIDE, 2, mesh.shape["batch"]), ("x", "y", "c", "z")
    )
    return jax.shard_map(
        body,
        mesh=torus,
        in_specs=(
            P("z", SEQ, None),
            P("z", SEQ, None),
            P("z", SEQ, None),
            P("z", SEQ),
            P("z", SEQ, None),
            P("z", None),
        ),
        out_specs=(P("z", SEQ, None), P("z", None)),
        check_vma=False,
    )
```

```python
import math

import jax
import jax.numpy as jnp
from jax import lax
from jax.experimental import pallas as pl
from jax.experimental.pallas import tpu as pltpu
from jax.sharding import Mesh
from jax.sharding import PartitionSpec as P

MESH = pl.DeviceIdType.MESH
SEQ = ("x", "y", "c")
F32 = jnp.float32
BF16 = jnp.bfloat16
SIDE = 4
CHIPS = SIDE * SIDE
LAYERS = 16
TILE = 8
TOKENS = 512
WIDTH = 256
HALF = 128
GROUPS = 6
COLS = 256
BOTH = 2 * TOKENS
PIPES = 2
UNITS = HALF // PIPES
HEIGHT = 3 * UNITS
TILES = 2 * HEIGHT // TILE
OWNED = TILES // CHIPS
NEAR = 4


def far_first():
    hops = lambda step: min(step, SIDE - step)
    steps = [(dx, dy) for dx in range(SIDE) for dy in range(SIDE) if dx or dy]
    return sorted(steps, key=lambda s: -(hops(s[0]) + hops(s[1])))


PEERS = far_first()
NPEERS = len(PEERS)
Z_STEPS = [d for dz in range(NEAR, 0, -1) for d in (dz, LAYERS - dz)]


def split(value):
    high = value.astype(BF16)
    return high, (value - high.astype(F32)).astype(BF16)


def dot(a, b):
    return jnp.dot(a, b, preferred_element_type=F32)


def kernel(
    q_in, k_in, v_in, rates_in, cot_in, w_in,
    out_ref, grad_ref,
    tok, mine, theirs, tok_b, tok_t, rates_own, rates_other, eta, w_own,
    natural, n_part, n_parts, n_chunk, n_adj,
    whole, part, parts, chunk,
    lhs_ab, lhs_c,
    pre_p, pre_g, pre_u, c1, c2, c3, c4,
    d_pair, e_pair, out_own, out_part, out_other, z_parts, z_sum, tail,
    load_sem, x_send, x_recv, r_send, r_recv, o_send, o_recv,
    n_send, n_recv, rs_send, rs_recv, ag_send, ag_recv,
    z_send, z_recv, zz_send, y_send, y_recv, t_send, t_recv,
):
    x, y, c, z = (lax.axis_index(name) for name in ("x", "y", "c", "z"))
    me = x * SIDE + y
    other = (x, y, 1 - c, z)

    loads = [
        pltpu.make_async_copy(src.at[0], tok.at[i], load_sem.at[i])
        for i, src in enumerate((k_in, v_in, q_in, cot_in))
    ]
    loads.append(pltpu.make_async_copy(rates_in, rates_own, load_sem.at[4]))
    for load in loads:
        load.start()

    def peer(step):
        px = lax.rem(x + step[0], SIDE)
        py = lax.rem(y + step[1], SIDE)
        return (px, py, c, z), px * SIDE + py

    def z_peer(dz):
        return (x, y, c, lax.rem(z + dz, LAYERS))

    peers = [peer(step) for step in PEERS]
    everyone = [(d[0], d[1], core, z) for d, _ in peers for core in (c, 1 - c)] + [other]

    barrier = pltpu.get_barrier_semaphore()
    greeted = [z_peer(dz) for dz in Z_STEPS] + everyone
    for device in greeted:
        pl.semaphore_signal(barrier, inc=1, device_id=device, device_id_type=MESH)

    for half in range(2):
        @pl.when(c == half)
        def _():
            w_own[...] = w_in[:, half * HALF : (half + 1) * HALF].reshape(GROUPS, TILE, HALF)

    divisor = math.sqrt(lax.axis_size(SEQ) * TOKENS)
    for load in loads:
        load.wait()
    for i in range(4):
        mine[i] = tok[i].astype(F32)
    eta[:, 0:TOKENS] = jnp.broadcast_to(-(rates_own[...] / divisor), (TILE, TOKENS))

    pl.semaphore_wait(barrier, len(greeted))

    sub = lax.rem(me + GROUPS * LAYERS - GROUPS * z, CHIPS)
    group = GROUPS * z + sub
    at = lax.div(group, CHIPS)
    owner = sub < GROUPS

    def z_copy(i):
        return pltpu.make_async_remote_copy(
            w_own.at[sub], n_chunk.at[at], z_send.at[i], z_recv.at[at],
            device_id=z_peer(Z_STEPS[i]), device_id_type=MESH,
        )

    @pl.when(owner)
    def _():
        for i in range(len(Z_STEPS)):
            z_copy(i).start()
        n_chunk[pl.ds(at, 1)] = w_own[pl.ds(sub, 1)]

    swaps = [
        pltpu.make_async_remote_copy(
            mine.at[i], theirs.at[i], x_send.at[i], x_recv.at[i], device_id=other, device_id_type=MESH
        )
        for i in range(4)
    ]
    swaps.append(
        pltpu.make_async_remote_copy(
            rates_own, rates_other, r_send, r_recv, device_id=other, device_id_type=MESH
        )
    )
    for swap in swaps:
        swap.start()

    def own_tokens(i):
        tok_b[i, 0:TOKENS] = tok[i]
        tok_t[i, :, 0:TOKENS] = mine[i].T.astype(BF16)

    def other_tokens(i):
        swaps[i].wait()
        tok_b[i, TOKENS:BOTH] = theirs[i].astype(BF16)
        tok_t[i, :, TOKENS:BOTH] = theirs[i].T.astype(BF16)

    for i in range(2):
        own_tokens(i)

    def z_pass(j, steps):
        dz = NEAR if steps > 0 else LAYERS - NEAR
        return pltpu.make_async_remote_copy(
            n_chunk.at[j], n_chunk.at[j], zz_send.at[j], z_recv.at[j],
            device_id=z_peer(dz), device_id_type=MESH,
        )

    def z_away(j):
        return lax.rem(z + LAYERS - lax.div(CHIPS * j + me, GROUPS), LAYERS)

    def z_landed(j):
        pltpu.make_async_remote_copy(
            w_own.at[0], n_chunk.at[j], z_send.at[0], z_recv.at[j], device_id=other, device_id_type=MESH
        ).wait_recv()

    def up(j):
        return (z_away(j) >= 1) & (z_away(j) <= NEAR)

    def down(j):
        return z_away(j) >= LAYERS - NEAR + 1

    for j in range(GROUPS):
        @pl.when(up(j))
        def _():
            z_landed(j)
            z_pass(j, 1).start()

        @pl.when(down(j))
        def _():
            z_landed(j)
            z_pass(j, -1).start()

        @pl.when(z_away(j) == LAYERS - NEAR)
        def _():
            z_landed(j)

    for i in range(2):
        other_tokens(i)
    swaps[4].wait()
    eta[:, TOKENS:BOTH] = jnp.broadcast_to(-(rates_other[...] / divisor), (TILE, TOKENS))

    for j in range(GROUPS):
        @pl.when((z_away(j) > NEAR) & (z_away(j) < LAYERS - NEAR))
        def _():
            z_landed(j)

    firsts = [
        pltpu.make_async_remote_copy(
            n_chunk, natural.at[:, me], n_send.at[k], n_recv.at[k], device_id=device, device_id_type=MESH
        )
        for k, (device, _) in enumerate(peers)
    ]
    for copy in firsts:
        copy.start()
    natural[:, pl.ds(me, 1)] = n_chunk[...].reshape(GROUPS, 1, TILE, HALF)

    for i in (2, 3):
        own_tokens(i)
        other_tokens(i)

    @pl.when(owner)
    def _():
        for i in range(len(Z_STEPS)):
            z_copy(i).wait_send()

    for j in range(GROUPS):
        @pl.when(up(j))
        def _():
            z_pass(j, 1).wait_send()

        @pl.when(down(j))
        def _():
            z_pass(j, -1).wait_send()

    def gathering(stage, pipe):
        return [
            pltpu.make_async_remote_copy(
                chunk.at[pipe], whole.at[stage, pipe, :, me], ag_send.at[pipe, k], ag_recv.at[pipe, k],
                device_id=device, device_id_type=MESH,
            )
            for k, (device, _) in enumerate(peers)
        ]

    def scattering(pipe):
        return [
            pltpu.make_async_remote_copy(
                part.at[pipe, :, chip], parts.at[pipe, k], rs_send.at[pipe, k], rs_recv.at[pipe, k],
                device_id=device, device_id_type=MESH,
            )
            for k, (device, chip) in enumerate(peers)
        ]

    def reduced(pipe):
        for copy in scattering(pipe):
            copy.wait()
        total = part[pipe, :, pl.ds(me, 1)].reshape(OWNED, TILE, HALF)
        for k in range(NPEERS):
            total = total + parts[pipe, k]
        return total

    def gather(stage, pipe, value):
        chunk[pipe] = value
        for copy in gathering(stage, pipe):
            copy.start()
        whole[stage, pipe, :, pl.ds(me, 1)] = value.reshape(OWNED, 1, TILE, HALF)

    def gathered(stage, pipe):
        for copy in gathering(stage, pipe):
            copy.wait()

    def from_tiles(tiles):
        flat = tiles.reshape(TILES, TILE, HALF)
        left = flat[: TILES // 2].reshape(HEIGHT, HALF)
        right = flat[TILES // 2 :].reshape(HEIGHT, HALF)
        return jnp.concatenate([left, right], axis=1)

    def to_tiles(value):
        left = value[:, :HALF].reshape(TILES // 2, TILE, HALF)
        right = value[:, HALF:].reshape(TILES // 2, TILE, HALF)
        return jnp.concatenate([left, right], axis=0).reshape(OWNED, CHIPS, TILE, HALF)

    def weights(stage, pipe):
        high, low = split(from_tiles(whole[stage, pipe]))
        lhs_ab[0 : 2 * UNITS] = high[: 2 * UNITS]
        lhs_ab[2 * UNITS :] = low[: 2 * UNITS]
        lhs_c[0:UNITS] = high[2 * UNITS :]
        lhs_c[UNITS:] = low[2 * UNITS :]

    def projected(first, second, cols):
        pg = dot(lhs_ab[...], tok_t[first, :, cols])
        pg = pg[: 2 * UNITS] + pg[2 * UNITS :]
        uu = dot(lhs_c[...], tok_t[second, :, cols])
        return pg[:UNITS], pg[UNITS:], uu[:UNITS] + uu[UNITS:]

    def keep(cols, dp, dg, e, pipe):
        for i, value in enumerate((dp, dg)):
            high, low = split(value)
            d_pair[i * UNITS : (i + 1) * UNITS, cols] = high
            d_pair[(2 + i) * UNITS : (3 + i) * UNITS, cols] = low
        high, low = split(e)
        e_pair[pipe, 0:UNITS, cols] = high
        e_pair[pipe, UNITS:, cols] = low

    def contract(first, second, pipe):
        ab = dot(d_pair[...], tok_b[first])
        cc = dot(e_pair[pipe], tok_b[second])
        return jnp.concatenate(
            [ab[: 2 * UNITS] + ab[2 * UNITS :], cc[:UNITS] + cc[UNITS:]], axis=0
        )

    def scatter(pipe, value):
        part[pipe] = to_tiles(value)
        for copy in scattering(pipe):
            copy.start()

    def token_loop(body):
        for i in range(BOTH // COLS):
            body(slice(i * COLS, (i + 1) * COLS))

    def sigmoid(g):
        return 1.0 / (1.0 + jnp.exp(-g))

    def rates(cols):
        return jnp.concatenate([eta[:, cols]] * (UNITS // TILE), axis=0)

    def inner(stage, pipe):
        weights(stage, pipe)

        def body(cols):
            p, g, u = projected(0, 1, cols)
            s = sigmoid(g)
            act = g * s
            slope = s + act * (1.0 - s)
            rate = rates(cols)
            f1 = rate * act
            f3 = rate * p * slope
            pre_p[pipe, :, cols] = p
            pre_g[pipe, :, cols] = g
            pre_u[pipe, :, cols] = u
            c1[stage, pipe, :, cols] = f1
            c3[stage, pipe, :, cols] = f3
            keep(cols, f1 * u, f3 * u, f1 * p, pipe)

        token_loop(body)
        return contract(0, 1, pipe)

    def inner_second(stage, pipe):
        def body(cols):
            p, g, u = pre_p[pipe, :, cols], pre_g[pipe, :, cols], pre_u[pipe, :, cols]
            s = sigmoid(g)
            slope = s + g * s * (1.0 - s)
            bend = s * (1.0 - s) * (2.0 + g * (1.0 - 2.0 * s))
            w = rates(cols) * u
            c2[stage, pipe, :, cols] = w * slope
            c4[stage, pipe, :, cols] = w * p * bend

        token_loop(body)

    def outer(pipe):
        weights(2, pipe)

        def body(cols):
            p, g, u = projected(2, 3, cols)
            s = sigmoid(g)
            act = g * s
            slope = s + act * (1.0 - s)
            keep(cols, u * act, u * p * slope, act * p, pipe)

        token_loop(body)
        return contract(2, 3, pipe)

    def hessian(stage, direction, pipe):
        weights(direction, pipe)

        def body(cols):
            p, g, u = projected(0, 1, cols)
            f1, f2 = c1[stage, pipe, :, cols], c2[stage, pipe, :, cols]
            f3, f4 = c3[stage, pipe, :, cols], c4[stage, pipe, :, cols]
            keep(cols, f1 * u + f2 * g, f3 * u + f2 * p + f4 * g, f3 * g + f1 * p, pipe)

        token_loop(body)
        return contract(0, 1, pipe)

    for copy in firsts:
        copy.wait()
    flipped = [
        natural[2 * i : 2 * i + 2].reshape(WIDTH, HALF).T for i in range(3)
    ]
    for pipe in range(PIPES):
        rows = slice(pipe * UNITS, (pipe + 1) * UNITS)
        whole[0, pipe] = to_tiles(jnp.concatenate([matrix[rows] for matrix in flipped], axis=0))

    def mine_of(stage, pipe):
        return whole[stage, pipe, :, pl.ds(me, 1)].reshape(OWNED, TILE, HALF)

    for pipe in range(PIPES):
        scatter(pipe, inner(0, pipe))
    for pipe in range(PIPES):
        inner_second(0, pipe)
    for pipe in range(PIPES):
        gather(1, pipe, mine_of(0, pipe) - reduced(pipe))
    for pipe in range(PIPES):
        gathered(1, pipe)
        scatter(pipe, inner(1, pipe))
    for pipe in range(PIPES):
        inner_second(1, pipe)
    for pipe in range(PIPES):
        gather(2, pipe, mine_of(1, pipe) - reduced(pipe))

    for pipe in range(PIPES):
        gathered(2, pipe)
        scatter(pipe, outer(pipe))

    def partial_out(cols):
        total = None
        for pipe in range(PIPES):
            ct_high, ct_low = split(from_tiles(whole[2, pipe])[2 * UNITS :])
            high = e_pair[pipe, 0:UNITS, cols].astype(F32).T.astype(BF16)
            low = e_pair[pipe, UNITS:, cols].astype(F32).T.astype(BF16)
            term = dot(high, ct_high) + (dot(high, ct_low) + dot(low, ct_high))
            total = term if total is None else total + term
        return total

    out_part[...] = partial_out(slice(TOKENS, BOTH))
    swap = pltpu.make_async_remote_copy(
        out_part, out_other, o_send, o_recv, device_id=other, device_id_type=MESH
    )
    swap.start()
    out_own[...] = partial_out(slice(0, TOKENS))
    for pipe in range(PIPES):
        gather(3, pipe, reduced(pipe))
    swap.wait()
    out_ref[0] = (out_own[...] + out_other[...]).astype(BF16)

    for pipe in range(PIPES):
        gathered(3, pipe)
        scatter(pipe, hessian(1, 3, pipe))
    for pipe in range(PIPES):
        gather(4, pipe, mine_of(3, pipe) - reduced(pipe))

    def upright(values):
        for i in range(3):
            rows = slice(i * UNITS, (i + 1) * UNITS)
            matrix = jnp.concatenate([value[rows] for value in values], axis=0)
            yield matrix.T.reshape(2, CHIPS, TILE, HALF)

    terms = []
    for pipe in range(PIPES):
        gathered(4, pipe)
        terms.append(hessian(0, 4, pipe))
    for i, value in enumerate(upright(terms)):
        n_part[2 * i : 2 * i + 2] = value
    lasts = [
        pltpu.make_async_remote_copy(
            n_part.at[:, chip], n_parts.at[k], n_send.at[k], n_recv.at[k],
            device_id=device, device_id_type=MESH,
        )
        for k, (device, chip) in enumerate(peers)
    ]
    for copy in lasts:
        copy.start()
    for i, value in enumerate(upright([from_tiles(whole[4, pipe]) for pipe in range(PIPES)])):
        n_adj[2 * i : 2 * i + 2] = value
    total = (n_adj[:, pl.ds(me, 1)] - n_part[:, pl.ds(me, 1)]).reshape(GROUPS, TILE, HALF)
    for copy in lasts:
        copy.wait()
    for k in range(NPEERS):
        total = total - n_parts[k]
    n_chunk[...] = total

    def to_owner(j):
        target = lax.div(CHIPS * j + me, GROUPS)
        slot = lax.rem(target + LAYERS - z, LAYERS)
        return target, pltpu.make_async_remote_copy(
            n_chunk.at[j], z_parts.at[slot], y_send.at[j], y_recv.at[slot],
            device_id=(x, y, c, target), device_id_type=MESH,
        )

    for j in range(GROUPS):
        target, copy = to_owner(j)

        @pl.when(target != z)
        def _():
            copy.start()

    def spread():
        return [
            pltpu.make_async_remote_copy(
                z_sum, tail.at[c, sub], t_send.at[k], t_recv.at[c, sub],
                device_id=device, device_id_type=MESH,
            )
            for k, device in enumerate(everyone)
        ]

    @pl.when(owner)
    def _():
        for slot in range(1, LAYERS):
            pltpu.make_async_remote_copy(
                n_chunk.at[0], z_parts.at[slot], y_send.at[0], y_recv.at[slot],
                device_id=other, device_id_type=MESH,
            ).wait_recv()
        total = n_chunk[pl.ds(at, 1)].reshape(TILE, HALF)
        for slot in range(1, LAYERS):
            total = total + z_parts[slot]
        z_sum[...] = total
        for copy in spread():
            copy.start()
        tail[pl.ds(c, 1), pl.ds(sub, 1)] = total.reshape(1, 1, TILE, HALF)

    for j in range(GROUPS):
        target, copy = to_owner(j)

        @pl.when(target != z)
        def _():
            copy.wait_send()

    for s in range(GROUPS):
        source = lax.rem(GROUPS * z + s, CHIPS)
        for core in range(2):

            @pl.when((source != me) | (c != core))
            def _():
                pltpu.make_async_remote_copy(
                    z_sum, tail.at[core, s], t_send.at[0], t_recv.at[core, s],
                    device_id=other, device_id_type=MESH,
                ).wait_recv()

    @pl.when(owner)
    def _():
        for copy in spread():
            copy.wait_send()

    for half in range(2):
        grad_ref[:, half * HALF : (half + 1) * HALF] = tail[half].reshape(GROUPS * TILE, HALF)


def body(queries, key_rows, value_rows, step_rates, cotangent, fast_init):
    vmem = lambda *shape: pltpu.VMEM(shape, F32)
    half = lambda *shape: pltpu.VMEM(shape, BF16)
    dma = lambda *shape: pltpu.SemaphoreType.DMA(shape)
    any_spec = pl.BlockSpec(memory_space=pl.ANY)
    vmem_spec = pl.BlockSpec(memory_space=pltpu.VMEM)
    return pl.pallas_call(
        kernel,
        out_shape=(
            jax.ShapeDtypeStruct(queries.shape, BF16),
            jax.ShapeDtypeStruct(fast_init.shape, F32),
        ),
        in_specs=[any_spec] * 5 + [vmem_spec],
        out_specs=(vmem_spec, vmem_spec),
        scratch_shapes=[
            half(4, TOKENS, WIDTH),
            vmem(4, TOKENS, WIDTH),
            vmem(4, TOKENS, WIDTH),
            half(4, BOTH, WIDTH),
            half(4, WIDTH, BOTH),
            vmem(1, TOKENS),
            vmem(1, TOKENS),
            vmem(TILE, BOTH),
            vmem(GROUPS, TILE, HALF),
            vmem(GROUPS, CHIPS, TILE, HALF),
            vmem(GROUPS, CHIPS, TILE, HALF),
            vmem(NPEERS, GROUPS, TILE, HALF),
            vmem(GROUPS, TILE, HALF),
            vmem(GROUPS, CHIPS, TILE, HALF),
            vmem(5, PIPES, OWNED, CHIPS, TILE, HALF),
            vmem(PIPES, OWNED, CHIPS, TILE, HALF),
            vmem(PIPES, NPEERS, OWNED, TILE, HALF),
            vmem(PIPES, OWNED, TILE, HALF),
            half(4 * UNITS, WIDTH),
            half(2 * UNITS, WIDTH),
            vmem(PIPES, UNITS, BOTH),
            vmem(PIPES, UNITS, BOTH),
            vmem(PIPES, UNITS, BOTH),
            vmem(2, PIPES, UNITS, BOTH),
            vmem(2, PIPES, UNITS, BOTH),
            vmem(2, PIPES, UNITS, BOTH),
            vmem(2, PIPES, UNITS, BOTH),
            half(4 * UNITS, BOTH),
            half(PIPES, 2 * UNITS, BOTH),
            vmem(TOKENS, WIDTH),
            vmem(TOKENS, WIDTH),
            vmem(TOKENS, WIDTH),
            vmem(LAYERS, TILE, HALF),
            vmem(TILE, HALF),
            vmem(2, GROUPS, TILE, HALF),
            dma(5),
            dma(4), dma(4),
            pltpu.SemaphoreType.DMA, pltpu.SemaphoreType.DMA,
            pltpu.SemaphoreType.DMA, pltpu.SemaphoreType.DMA,
            dma(NPEERS), dma(NPEERS),
            dma(PIPES, NPEERS), dma(PIPES, NPEERS),
            dma(PIPES, NPEERS), dma(PIPES, NPEERS),
            dma(len(Z_STEPS)), dma(GROUPS), dma(GROUPS),
            dma(GROUPS), dma(LAYERS),
            dma(2 * NPEERS + 1), dma(2, GROUPS),
        ],
        compiler_params=pltpu.CompilerParams(
            collective_id=0, has_side_effects=True, vmem_limit_bytes=56 * 2**20
        ),
    )(queries, key_rows, value_rows, step_rates, cotangent, fast_init)


def solution(mesh):
    torus = Mesh(
        mesh.devices.reshape(SIDE, SIDE, 2, mesh.shape["batch"]), ("x", "y", "c", "z")
    )
    return jax.shard_map(
        body,
        mesh=torus,
        in_specs=(
            P("z", SEQ, None),
            P("z", SEQ, None),
            P("z", SEQ, None),
            P("z", SEQ),
            P("z", SEQ, None),
            P("z", None),
        ),
        out_specs=(P("z", SEQ, None), P("z", None)),
        check_vma=False,
    )
```

```python
import math

import jax
import jax.numpy as jnp
from jax import lax
from jax.experimental import pallas as pl
from jax.experimental.pallas import tpu as pltpu
from jax.sharding import Mesh
from jax.sharding import PartitionSpec as P

MESH = pl.DeviceIdType.MESH
SEQ = ("x", "y", "c")
F32 = jnp.float32
BF16 = jnp.bfloat16
SIDE = 4
CHIPS = SIDE * SIDE
LAYERS = 16
TILE = 8
TOKENS = 512
WIDTH = 256
HALF = 128
GROUPS = 6
COLS = 256
BOTH = 2 * TOKENS
PIPES = 2
UNITS = HALF // PIPES
HEIGHT = 3 * UNITS
TILES = 2 * HEIGHT // TILE
OWNED = TILES // CHIPS
NEAR = 4


def far_first():
    hops = lambda step: min(step, SIDE - step)
    steps = [(dx, dy) for dx in range(SIDE) for dy in range(SIDE) if dx or dy]
    return sorted(steps, key=lambda s: -(hops(s[0]) + hops(s[1])))


PEERS = far_first()
NPEERS = len(PEERS)
Z_STEPS = [d for dz in range(NEAR, 0, -1) for d in (dz, LAYERS - dz)]


def split(value):
    high = value.astype(BF16)
    return high, (value - high.astype(F32)).astype(BF16)


def dot(a, b):
    return jnp.dot(a, b, preferred_element_type=F32)


def kernel(
    q_in, k_in, v_in, rates_in, cot_in, w_in,
    out_ref, grad_ref,
    tok, mine, theirs, tok_b, tok_t, rates_own, rates_other, eta, w_own,
    natural, n_part, n_parts, n_chunk, n_adj,
    whole, part, parts, chunk,
    lhs_ab, lhs_c,
    pre_p, pre_g, pre_u, c1, c2, c3, c4,
    d_pair, e_pair, out_own, out_part, out_other, z_parts, z_sum, tail, waits, out_final,
    load_sem, x_send, x_recv, r_send, r_recv, o_send, o_recv,
    n_send, n_recv, rs_send, rs_recv, ag_send, ag_recv,
    z_send, z_recv, zz_send, y_send, y_recv, t_send, t_recv, out_sem, grad_sem,
):
    x, y, c, z = (lax.axis_index(name) for name in ("x", "y", "c", "z"))
    me = x * SIDE + y
    other = (x, y, 1 - c, z)

    def peer(step):
        px = lax.rem(x + step[0], SIDE)
        py = lax.rem(y + step[1], SIDE)
        return (px, py, c, z), px * SIDE + py

    def z_peer(dz):
        return (x, y, c, lax.rem(z + dz, LAYERS))

    peers = [peer(step) for step in PEERS]
    everyone = [(d[0], d[1], core, z) for d, _ in peers for core in (c, 1 - c)] + [other]

    barrier = pltpu.get_barrier_semaphore()
    greeted = [z_peer(dz) for dz in Z_STEPS] + everyone
    for device in greeted:
        pl.semaphore_signal(barrier, inc=1, device_id=device, device_id_type=MESH)

    loads = [
        pltpu.make_async_copy(src.at[0], tok.at[i], load_sem.at[i])
        for i, src in enumerate((k_in, v_in, q_in, cot_in))
    ]
    loads.append(pltpu.make_async_copy(rates_in, rates_own, load_sem.at[4]))
    for half in range(2):
        @pl.when(c == half)
        def _():
            pltpu.make_async_copy(
                w_in.at[:, :, half * HALF : (half + 1) * HALF], w_own, load_sem.at[5]
            ).start()
    for load in loads:
        load.start()

    divisor = math.sqrt(lax.axis_size(SEQ) * TOKENS)
    for load in loads:
        load.wait()
    for i in range(4):
        mine[i] = tok[i].astype(F32)
    eta[:, 0:TOKENS] = jnp.broadcast_to(-(rates_own[...] / divisor), (TILE, TOKENS))

    pltpu.make_async_copy(w_own, w_own, load_sem.at[5]).wait()
    pl.semaphore_wait(barrier, len(greeted))

    sub = lax.rem(me + GROUPS * LAYERS - GROUPS * z, CHIPS)
    group = GROUPS * z + sub
    at = lax.div(group, CHIPS)
    owner = sub < GROUPS

    def z_copy(i):
        return pltpu.make_async_remote_copy(
            w_own.at[sub], n_chunk.at[at], z_send.at[i], z_recv.at[at],
            device_id=z_peer(Z_STEPS[i]), device_id_type=MESH,
        )

    @pl.when(owner)
    def _():
        for i in range(len(Z_STEPS)):
            z_copy(i).start()
        n_chunk[pl.ds(at, 1)] = w_own[pl.ds(sub, 1)]

    swaps = [
        pltpu.make_async_remote_copy(
            mine.at[i], theirs.at[i], x_send.at[i], x_recv.at[i], device_id=other, device_id_type=MESH
        )
        for i in range(4)
    ]
    swaps.append(
        pltpu.make_async_remote_copy(
            rates_own, rates_other, r_send, r_recv, device_id=other, device_id_type=MESH
        )
    )
    for swap in swaps:
        swap.start()

    def own_tokens(i):
        tok_b[i, 0:TOKENS] = tok[i]
        tok_t[i, :, 0:TOKENS] = mine[i].T.astype(BF16)

    def other_tokens(i):
        swaps[i].wait()
        tok_b[i, TOKENS:BOTH] = theirs[i].astype(BF16)
        tok_t[i, :, TOKENS:BOTH] = theirs[i].T.astype(BF16)

    for i in range(2):
        own_tokens(i)

    def z_pass(j, steps):
        dz = NEAR if steps > 0 else LAYERS - NEAR
        return pltpu.make_async_remote_copy(
            n_chunk.at[j], n_chunk.at[j], zz_send.at[j], z_recv.at[j],
            device_id=z_peer(dz), device_id_type=MESH,
        )

    def z_away(j):
        return lax.rem(z + LAYERS - lax.div(CHIPS * j + me, GROUPS), LAYERS)

    def z_landed(j):
        pltpu.make_async_remote_copy(
            w_own.at[0], n_chunk.at[j], z_send.at[0], z_recv.at[j], device_id=other, device_id_type=MESH
        ).wait_recv()

    def up(j):
        return (z_away(j) >= 1) & (z_away(j) <= NEAR)

    def down(j):
        return z_away(j) >= LAYERS - NEAR + 1

    for j in range(GROUPS):
        @pl.when(up(j))
        def _():
            z_landed(j)
            z_pass(j, 1).start()

        @pl.when(down(j))
        def _():
            z_landed(j)
            z_pass(j, -1).start()

        @pl.when(z_away(j) == LAYERS - NEAR)
        def _():
            z_landed(j)

    def pass_round(j):
        for device, _ in peers:
            pltpu.make_async_remote_copy(
                n_chunk.at[j], natural.at[j, me], n_send, n_recv, device_id=device, device_id_type=MESH
            ).start()
        natural[j, pl.ds(me, 1)] = n_chunk[pl.ds(j, 1)]

    def far(j):
        return (z_away(j) > NEAR) & (z_away(j) < LAYERS - NEAR)

    for j in range(GROUPS):
        @pl.when((z_away(j) <= NEAR) | (z_away(j) >= LAYERS - NEAR))
        def _():
            pass_round(j)

    for i in range(2):
        other_tokens(i)
    swaps[4].wait()
    eta[:, TOKENS:BOTH] = jnp.broadcast_to(-(rates_other[...] / divisor), (TILE, TOKENS))

    for j in range(GROUPS):
        @pl.when(far(j))
        def _():
            z_landed(j)
            pass_round(j)

    for i in (2, 3):
        own_tokens(i)
        other_tokens(i)

    @pl.when(owner)
    def _():
        for i in range(len(Z_STEPS)):
            z_copy(i).wait_send()

    for j in range(GROUPS):
        @pl.when(up(j))
        def _():
            z_pass(j, 1).wait_send()

        @pl.when(down(j))
        def _():
            z_pass(j, -1).wait_send()

    def all_of(landed, semaphore):
        pltpu.make_async_copy(landed, landed, semaphore).wait()

    def gathering(stage, pipe):
        return [
            pltpu.make_async_remote_copy(
                chunk.at[pipe], whole.at[stage, pipe, :, me], ag_send.at[pipe], ag_recv.at[pipe],
                device_id=device, device_id_type=MESH,
            )
            for device, _ in peers
        ]

    def scattering(pipe):
        return [
            pltpu.make_async_remote_copy(
                part.at[pipe, :, chip], parts.at[pipe, k], rs_send.at[pipe], rs_recv.at[pipe],
                device_id=device, device_id_type=MESH,
            )
            for k, (device, chip) in enumerate(peers)
        ]

    def reduced(pipe):
        all_of(parts.at[pipe], rs_recv.at[pipe])
        total = part[pipe, :, pl.ds(me, 1)].reshape(OWNED, TILE, HALF)
        for k in range(NPEERS):
            total = total + parts[pipe, k]
        return total

    def gather(stage, pipe, value):
        chunk[pipe] = value
        for copy in gathering(stage, pipe):
            copy.start()
        whole[stage, pipe, :, pl.ds(me, 1)] = value.reshape(OWNED, 1, TILE, HALF)
        all_of(parts.at[pipe], rs_send.at[pipe])

    def gathered(stage, pipe):
        all_of(whole.at[stage, pipe, :, pl.ds(0, NPEERS)], ag_recv.at[pipe])
        all_of(parts.at[pipe], ag_send.at[pipe])

    def from_tiles(tiles):
        flat = tiles.reshape(TILES, TILE, HALF)
        left = flat[: TILES // 2].reshape(HEIGHT, HALF)
        right = flat[TILES // 2 :].reshape(HEIGHT, HALF)
        return jnp.concatenate([left, right], axis=1)

    def to_tiles(value):
        left = value[:, :HALF].reshape(TILES // 2, TILE, HALF)
        right = value[:, HALF:].reshape(TILES // 2, TILE, HALF)
        return jnp.concatenate([left, right], axis=0).reshape(OWNED, CHIPS, TILE, HALF)

    def weights(stage, pipe):
        high, low = split(from_tiles(whole[stage, pipe]))
        lhs_ab[0 : 2 * UNITS] = high[: 2 * UNITS]
        lhs_ab[2 * UNITS :] = low[: 2 * UNITS]
        lhs_c[0:UNITS] = high[2 * UNITS :]
        lhs_c[UNITS:] = low[2 * UNITS :]

    def projected(first, second, cols):
        pg = dot(lhs_ab[...], tok_t[first, :, cols])
        pg = pg[: 2 * UNITS] + pg[2 * UNITS :]
        uu = dot(lhs_c[...], tok_t[second, :, cols])
        return pg[:UNITS], pg[UNITS:], uu[:UNITS] + uu[UNITS:]

    def keep(cols, dp, dg, e, pipe):
        for i, value in enumerate((dp, dg)):
            high, low = split(value)
            d_pair[i * UNITS : (i + 1) * UNITS, cols] = high
            d_pair[(2 + i) * UNITS : (3 + i) * UNITS, cols] = low
        high, low = split(e)
        e_pair[pipe, 0:UNITS, cols] = high
        e_pair[pipe, UNITS:, cols] = low

    def contract(first, second, pipe):
        ab = dot(d_pair[...], tok_b[first])
        cc = dot(e_pair[pipe], tok_b[second])
        return jnp.concatenate(
            [ab[: 2 * UNITS] + ab[2 * UNITS :], cc[:UNITS] + cc[UNITS:]], axis=0
        )

    def scatter(pipe, value):
        part[pipe] = to_tiles(value)
        for copy in scattering(pipe):
            copy.start()

    def token_loop(body):
        for i in range(BOTH // COLS):
            body(slice(i * COLS, (i + 1) * COLS))

    def sigmoid(g):
        return 1.0 / (1.0 + jnp.exp(-g))

    def rates(cols):
        return jnp.concatenate([eta[:, cols]] * (UNITS // TILE), axis=0)

    def inner(stage, pipe):
        weights(stage, pipe)

        def body(cols):
            p, g, u = projected(0, 1, cols)
            s = sigmoid(g)
            act = g * s
            slope = s + act * (1.0 - s)
            rate = rates(cols)
            f1 = rate * act
            f3 = rate * p * slope
            pre_p[pipe, :, cols] = p
            pre_g[pipe, :, cols] = g
            pre_u[pipe, :, cols] = u
            c1[stage, pipe, :, cols] = f1
            c3[stage, pipe, :, cols] = f3
            keep(cols, f1 * u, f3 * u, f1 * p, pipe)

        token_loop(body)
        return contract(0, 1, pipe)

    def inner_second(stage, pipe):
        def body(cols):
            p, g, u = pre_p[pipe, :, cols], pre_g[pipe, :, cols], pre_u[pipe, :, cols]
            s = sigmoid(g)
            slope = s + g * s * (1.0 - s)
            bend = s * (1.0 - s) * (2.0 + g * (1.0 - 2.0 * s))
            w = rates(cols) * u
            c2[stage, pipe, :, cols] = w * slope
            c4[stage, pipe, :, cols] = w * p * bend

        token_loop(body)

    def outer(pipe):
        weights(2, pipe)

        def body(cols):
            p, g, u = projected(2, 3, cols)
            s = sigmoid(g)
            act = g * s
            slope = s + act * (1.0 - s)
            keep(cols, u * act, u * p * slope, act * p, pipe)

        token_loop(body)
        return contract(2, 3, pipe)

    def hessian(stage, direction, pipe):
        weights(direction, pipe)

        def body(cols):
            p, g, u = projected(0, 1, cols)
            f1, f2 = c1[stage, pipe, :, cols], c2[stage, pipe, :, cols]
            f3, f4 = c3[stage, pipe, :, cols], c4[stage, pipe, :, cols]
            keep(cols, f1 * u + f2 * g, f3 * u + f2 * p + f4 * g, f3 * g + f1 * p, pipe)

        token_loop(body)
        return contract(0, 1, pipe)

    all_of(natural.at[:, pl.ds(0, NPEERS)], n_recv)
    all_of(n_parts, n_send)
    flipped = [
        natural[2 * i : 2 * i + 2].reshape(WIDTH, HALF).T for i in range(3)
    ]
    for pipe in range(PIPES):
        rows = slice(pipe * UNITS, (pipe + 1) * UNITS)
        whole[0, pipe] = to_tiles(jnp.concatenate([matrix[rows] for matrix in flipped], axis=0))

    def mine_of(stage, pipe):
        return whole[stage, pipe, :, pl.ds(me, 1)].reshape(OWNED, TILE, HALF)

    for pipe in range(PIPES):
        scatter(pipe, inner(0, pipe))
    for pipe in range(PIPES):
        inner_second(0, pipe)
    for pipe in range(PIPES):
        gather(1, pipe, mine_of(0, pipe) - reduced(pipe))
    for pipe in range(PIPES):
        gathered(1, pipe)
        scatter(pipe, inner(1, pipe))
    for pipe in range(PIPES):
        inner_second(1, pipe)
    for pipe in range(PIPES):
        gather(2, pipe, mine_of(1, pipe) - reduced(pipe))

    for pipe in range(PIPES):
        gathered(2, pipe)
        scatter(pipe, outer(pipe))

    def partial_out(cols):
        total = None
        for pipe in range(PIPES):
            ct_high, ct_low = split(from_tiles(whole[2, pipe])[2 * UNITS :])
            high = e_pair[pipe, 0:UNITS, cols].astype(F32).T.astype(BF16)
            low = e_pair[pipe, UNITS:, cols].astype(F32).T.astype(BF16)
            term = dot(high, ct_high) + (dot(high, ct_low) + dot(low, ct_high))
            total = term if total is None else total + term
        return total

    out_part[...] = partial_out(slice(TOKENS, BOTH))
    swap = pltpu.make_async_remote_copy(
        out_part, out_other, o_send, o_recv, device_id=other, device_id_type=MESH
    )
    swap.start()
    out_own[...] = partial_out(slice(0, TOKENS))
    for pipe in range(PIPES):
        gather(3, pipe, reduced(pipe))
    swap.wait()
    out_final[...] = (out_own[...] + out_other[...]).astype(BF16)
    out_copy = pltpu.make_async_copy(out_final, out_ref.at[0], out_sem)
    out_copy.start()

    for pipe in range(PIPES):
        gathered(3, pipe)
        scatter(pipe, hessian(1, 3, pipe))
    for pipe in range(PIPES):
        gather(4, pipe, mine_of(3, pipe) - reduced(pipe))

    def upright(values):
        for i in range(3):
            rows = slice(i * UNITS, (i + 1) * UNITS)
            matrix = jnp.concatenate([value[rows] for value in values], axis=0)
            yield matrix.T.reshape(2, CHIPS, TILE, HALF)

    terms = []
    for pipe in range(PIPES):
        gathered(4, pipe)
        terms.append(hessian(0, 4, pipe))
    for i, value in enumerate(upright(terms)):
        n_part[2 * i : 2 * i + 2] = value
    lasts = [
        pltpu.make_async_remote_copy(
            n_part.at[:, chip], n_parts.at[k], n_send, n_recv,
            device_id=device, device_id_type=MESH,
        )
        for k, (device, chip) in enumerate(peers)
    ]
    for copy in lasts:
        copy.start()
    for i, value in enumerate(upright([from_tiles(whole[4, pipe]) for pipe in range(PIPES)])):
        n_adj[2 * i : 2 * i + 2] = value
    total = (n_adj[:, pl.ds(me, 1)] - n_part[:, pl.ds(me, 1)]).reshape(GROUPS, TILE, HALF)
    all_of(n_parts, n_recv)
    for k in range(NPEERS):
        total = total - n_parts[k]
    n_chunk[...] = total

    def to_owner(j):
        target = lax.div(CHIPS * j + me, GROUPS)
        slot = lax.rem(target + LAYERS - z, LAYERS)
        return target, pltpu.make_async_remote_copy(
            n_chunk.at[j], z_parts.at[slot - 1], y_send.at[j], y_recv,
            device_id=(x, y, c, target), device_id_type=MESH,
        )

    for j in range(GROUPS):
        target, copy = to_owner(j)

        @pl.when(target != z)
        def _():
            copy.start()

    spread_bytes = waits.at[0 : len(everyone)]

    all_of(n_parts, n_send)

    def spread():
        return [
            pltpu.make_async_remote_copy(
                z_sum, tail.at[c, sub], t_send, t_recv.at[c, sub],
                device_id=device, device_id_type=MESH,
            )
            for device in everyone
        ]

    @pl.when(owner)
    def _():
        all_of(z_parts, y_recv)
        total = n_chunk[pl.ds(at, 1)].reshape(TILE, HALF)
        for slot in range(LAYERS - 1):
            total = total + z_parts[slot]
        z_sum[...] = total
        for copy in spread():
            copy.start()
        tail[pl.ds(c, 1), pl.ds(sub, 1)] = total.reshape(1, 1, TILE, HALF)

    for j in range(GROUPS):
        target, copy = to_owner(j)

        @pl.when(target != z)
        def _():
            copy.wait_send()

    for s in range(GROUPS):
        source = lax.rem(GROUPS * z + s, CHIPS)
        for core in range(2):

            @pl.when((source != me) | (c != core))
            def _():
                pltpu.make_async_remote_copy(
                    z_sum, tail.at[core, s], t_send, t_recv.at[core, s],
                    device_id=other, device_id_type=MESH,
                ).wait_recv()

    @pl.when(owner)
    def _():
        all_of(spread_bytes, t_send)

    grad_copies = [
        pltpu.make_async_copy(
            tail.at[half], grad_ref.at[:, :, half * HALF : (half + 1) * HALF], grad_sem.at[half]
        )
        for half in range(2)
    ]
    for copy in grad_copies:
        copy.start()
    out_copy.wait()
    for copy in grad_copies:
        copy.wait()


def body(queries, key_rows, value_rows, step_rates, cotangent, fast_init):
    vmem = lambda *shape: pltpu.VMEM(shape, F32)
    half = lambda *shape: pltpu.VMEM(shape, BF16)
    dma = lambda *shape: pltpu.SemaphoreType.DMA(shape)
    vmem_spec = pl.BlockSpec(memory_space=pltpu.VMEM)
    any_spec = pl.BlockSpec(memory_space=pl.ANY)
    result, grad = pl.pallas_call(
        kernel,
        out_shape=(
            pltpu.VMEM(queries.shape, BF16),
            pltpu.VMEM((GROUPS, TILE, WIDTH), F32),
        ),
        in_specs=[any_spec] * 6,
        out_specs=(vmem_spec, vmem_spec),
        scratch_shapes=[
            half(4, TOKENS, WIDTH),
            vmem(4, TOKENS, WIDTH),
            vmem(4, TOKENS, WIDTH),
            half(4, BOTH, WIDTH),
            half(4, WIDTH, BOTH),
            vmem(1, TOKENS),
            vmem(1, TOKENS),
            vmem(TILE, BOTH),
            vmem(GROUPS, TILE, HALF),
            vmem(GROUPS, CHIPS, TILE, HALF),
            vmem(GROUPS, CHIPS, TILE, HALF),
            vmem(NPEERS, GROUPS, TILE, HALF),
            vmem(GROUPS, TILE, HALF),
            vmem(GROUPS, CHIPS, TILE, HALF),
            vmem(5, PIPES, OWNED, CHIPS, TILE, HALF),
            vmem(PIPES, OWNED, CHIPS, TILE, HALF),
            vmem(PIPES, NPEERS, OWNED, TILE, HALF),
            vmem(PIPES, OWNED, TILE, HALF),
            half(4 * UNITS, WIDTH),
            half(2 * UNITS, WIDTH),
            vmem(PIPES, UNITS, BOTH),
            vmem(PIPES, UNITS, BOTH),
            vmem(PIPES, UNITS, BOTH),
            vmem(2, PIPES, UNITS, BOTH),
            vmem(2, PIPES, UNITS, BOTH),
            vmem(2, PIPES, UNITS, BOTH),
            vmem(2, PIPES, UNITS, BOTH),
            half(4 * UNITS, BOTH),
            half(PIPES, 2 * UNITS, BOTH),
            vmem(TOKENS, WIDTH),
            vmem(TOKENS, WIDTH),
            vmem(TOKENS, WIDTH),
            vmem(LAYERS - 1, TILE, HALF),
            vmem(TILE, HALF),
            vmem(2, GROUPS, TILE, HALF),
            vmem(2 * CHIPS, TILE, HALF),
            half(TOKENS, WIDTH),
            dma(6),
            dma(4), dma(4),
            pltpu.SemaphoreType.DMA, pltpu.SemaphoreType.DMA,
            pltpu.SemaphoreType.DMA, pltpu.SemaphoreType.DMA,
            pltpu.SemaphoreType.DMA, pltpu.SemaphoreType.DMA,
            dma(PIPES), dma(PIPES),
            dma(PIPES), dma(PIPES),
            dma(len(Z_STEPS)), dma(GROUPS), dma(GROUPS),
            dma(GROUPS), pltpu.SemaphoreType.DMA,
            pltpu.SemaphoreType.DMA, dma(2, GROUPS),
            pltpu.SemaphoreType.DMA, dma(2),
        ],
        compiler_params=pltpu.CompilerParams(
            collective_id=0, has_side_effects=True, vmem_limit_bytes=56 * 2**20
        ),
    )(queries, key_rows, value_rows, step_rates, cotangent, fast_init.reshape(GROUPS, TILE, WIDTH))
    return result, grad.reshape(fast_init.shape)


def solution(mesh):
    torus = Mesh(
        mesh.devices.reshape(SIDE, SIDE, 2, mesh.shape["batch"]), ("x", "y", "c", "z")
    )
    return jax.shard_map(
        body,
        mesh=torus,
        in_specs=(
            P("z", SEQ, None),
            P("z", SEQ, None),
            P("z", SEQ, None),
            P("z", SEQ),
            P("z", SEQ, None),
            P("z", None),
        ),
        out_specs=(P("z", SEQ, None), P("z", None)),
        check_vma=False,
    )
```

```python
import math

import jax
import jax.numpy as jnp
from jax import lax
from jax.experimental import pallas as pl
from jax.experimental.pallas import tpu as pltpu
from jax.sharding import Mesh
from jax.sharding import PartitionSpec as P

MESH = pl.DeviceIdType.MESH
SEQ = ("x", "y", "c")
F32 = jnp.float32
BF16 = jnp.bfloat16
SIDE = 4
CHIPS = SIDE * SIDE
LAYERS = 16
TILE = 8
TOKENS = 512
WIDTH = 256
HALF = 128
GROUPS = 6
COLS = 256
BOTH = 2 * TOKENS
PIPES = 2
UNITS = HALF // PIPES
HEIGHT = 3 * UNITS
TILES = 2 * HEIGHT // TILE
OWNED = TILES // CHIPS
STRIP = GROUPS * TILE // PIPES
SHARE = STRIP // TILE
NEAR = 4


def far_first():
    hops = lambda step: min(step, SIDE - step)
    steps = [(dx, dy) for dx in range(SIDE) for dy in range(SIDE) if dx or dy]
    return sorted(steps, key=lambda s: -(hops(s[0]) + hops(s[1])))


PEERS = far_first()
NPEERS = len(PEERS)
Z_STEPS = [d for dz in range(NEAR, 0, -1) for d in (dz, LAYERS - dz)]


def split(value):
    high = value.astype(BF16)
    return high, (value - high.astype(F32)).astype(BF16)


def dot(a, b):
    return jnp.dot(a, b, preferred_element_type=F32)


def kernel(
    q_in, k_in, v_in, rates_in, cot_in, w_in,
    out_ref, grad_ref,
    tok, mine, theirs, tok_b, tok_t, rates_own, rates_other, eta, w_own,
    natural, n_chunk, adj,
    whole, part, parts, chunk,
    lhs_ab, lhs_c,
    pre_p, pre_g, pre_u, c1, c2, c3, c4,
    d_pair, e_pair, out_own, out_part, out_other, z_parts, z_sum, tail, waits,
    load_sem, x_send, x_recv, r_send, r_recv, o_send, o_recv,
    n_send, n_recv, rs_send, rs_recv, ag_send, ag_recv,
    z_send, z_recv, zz_send, y_send, y_recv, t_send, t_recv,
):
    x, y, c, z = (lax.axis_index(name) for name in ("x", "y", "c", "z"))
    me = x * SIDE + y
    other = (x, y, 1 - c, z)

    def peer(step):
        px = lax.rem(x + step[0], SIDE)
        py = lax.rem(y + step[1], SIDE)
        return (px, py, c, z), px * SIDE + py

    def z_peer(dz):
        return (x, y, c, lax.rem(z + dz, LAYERS))

    peers = [peer(step) for step in PEERS]
    everyone = [(d[0], d[1], core, z) for d, _ in peers for core in (c, 1 - c)] + [other]

    barrier = pltpu.get_barrier_semaphore()
    greeted = [z_peer(dz) for dz in Z_STEPS] + everyone
    for device in greeted:
        pl.semaphore_signal(barrier, inc=1, device_id=device, device_id_type=MESH)

    loads = [
        pltpu.make_async_copy(src.at[0], tok.at[i], load_sem.at[i])
        for i, src in enumerate((k_in, v_in, q_in, cot_in))
    ]
    loads.append(pltpu.make_async_copy(rates_in, rates_own, load_sem.at[4]))
    for half in range(2):
        @pl.when(c == half)
        def _():
            pltpu.make_async_copy(
                w_in.at[:, :, half * HALF : (half + 1) * HALF], w_own, load_sem.at[5]
            ).start()
    for load in loads:
        load.start()

    divisor = math.sqrt(lax.axis_size(SEQ) * TOKENS)
    for load in loads:
        load.wait()
    for i in range(4):
        mine[i] = tok[i].astype(F32)
    eta[:, 0:TOKENS] = jnp.broadcast_to(-(rates_own[...] / divisor), (TILE, TOKENS))

    pltpu.make_async_copy(w_own, w_own, load_sem.at[5]).wait()
    pl.semaphore_wait(barrier, len(greeted))

    sub = lax.rem(me + GROUPS * LAYERS - GROUPS * z, CHIPS)
    group = GROUPS * z + sub
    at = lax.div(group, CHIPS)
    owner = sub < GROUPS

    def z_copy(i):
        return pltpu.make_async_remote_copy(
            w_own.at[sub], n_chunk.at[at], z_send.at[i], z_recv.at[at],
            device_id=z_peer(Z_STEPS[i]), device_id_type=MESH,
        )

    @pl.when(owner)
    def _():
        for i in range(len(Z_STEPS)):
            z_copy(i).start()
        n_chunk[pl.ds(at, 1)] = w_own[pl.ds(sub, 1)]

    swaps = [
        pltpu.make_async_remote_copy(
            mine.at[i], theirs.at[i], x_send.at[i], x_recv.at[i], device_id=other, device_id_type=MESH
        )
        for i in range(4)
    ]
    swaps.append(
        pltpu.make_async_remote_copy(
            rates_own, rates_other, r_send, r_recv, device_id=other, device_id_type=MESH
        )
    )
    for swap in swaps:
        swap.start()

    def own_tokens(i):
        tok_b[i, 0:TOKENS] = tok[i]
        tok_t[i, :, 0:TOKENS] = mine[i].T.astype(BF16)

    def other_tokens(i):
        swaps[i].wait()
        tok_b[i, TOKENS:BOTH] = theirs[i].astype(BF16)
        tok_t[i, :, TOKENS:BOTH] = theirs[i].T.astype(BF16)

    for i in range(2):
        own_tokens(i)

    def z_pass(j, steps):
        dz = NEAR if steps > 0 else LAYERS - NEAR
        return pltpu.make_async_remote_copy(
            n_chunk.at[j], n_chunk.at[j], zz_send.at[j], z_recv.at[j],
            device_id=z_peer(dz), device_id_type=MESH,
        )

    def z_away(j):
        return lax.rem(z + LAYERS - lax.div(CHIPS * j + me, GROUPS), LAYERS)

    def z_landed(j):
        pltpu.make_async_remote_copy(
            w_own.at[0], n_chunk.at[j], z_send.at[0], z_recv.at[j], device_id=other, device_id_type=MESH
        ).wait_recv()

    def up(j):
        return (z_away(j) >= 1) & (z_away(j) <= NEAR)

    def down(j):
        return z_away(j) >= LAYERS - NEAR + 1

    for j in range(GROUPS):
        @pl.when(up(j))
        def _():
            z_landed(j)
            z_pass(j, 1).start()

        @pl.when(down(j))
        def _():
            z_landed(j)
            z_pass(j, -1).start()

        @pl.when(z_away(j) == LAYERS - NEAR)
        def _():
            z_landed(j)

    def pass_round(j):
        for device, _ in peers:
            pltpu.make_async_remote_copy(
                n_chunk.at[j], natural.at[j, me], n_send, n_recv, device_id=device, device_id_type=MESH
            ).start()
        natural[j, pl.ds(me, 1)] = n_chunk[pl.ds(j, 1)]

    def far(j):
        return (z_away(j) > NEAR) & (z_away(j) < LAYERS - NEAR)

    for j in range(GROUPS):
        @pl.when((z_away(j) <= NEAR) | (z_away(j) >= LAYERS - NEAR))
        def _():
            pass_round(j)

    for i in range(2):
        other_tokens(i)
    swaps[4].wait()
    eta[:, TOKENS:BOTH] = jnp.broadcast_to(-(rates_other[...] / divisor), (TILE, TOKENS))

    for j in range(GROUPS):
        @pl.when(far(j))
        def _():
            z_landed(j)
            pass_round(j)

    for i in (2, 3):
        own_tokens(i)
        other_tokens(i)

    @pl.when(owner)
    def _():
        for i in range(len(Z_STEPS)):
            z_copy(i).wait_send()

    for j in range(GROUPS):
        @pl.when(up(j))
        def _():
            z_pass(j, 1).wait_send()

        @pl.when(down(j))
        def _():
            z_pass(j, -1).wait_send()

    def all_of(landed, semaphore):
        pltpu.make_async_copy(landed, landed, semaphore).wait()

    def gathering(stage, pipe):
        return [
            pltpu.make_async_remote_copy(
                chunk.at[pipe], whole.at[stage, pipe, :, me], ag_send.at[pipe], ag_recv.at[pipe],
                device_id=device, device_id_type=MESH,
            )
            for device, _ in peers
        ]

    def scattering(pipe):
        return [
            pltpu.make_async_remote_copy(
                part.at[pipe, :, chip], parts.at[pipe, k], rs_send.at[pipe], rs_recv.at[pipe],
                device_id=device, device_id_type=MESH,
            )
            for k, (device, chip) in enumerate(peers)
        ]

    def reduced(pipe):
        all_of(parts.at[pipe], rs_recv.at[pipe])
        total = part[pipe, :, pl.ds(me, 1)].reshape(OWNED, TILE, HALF)
        for k in range(NPEERS):
            total = total + parts[pipe, k]
        return total

    def gather(stage, pipe, value):
        chunk[pipe] = value
        for copy in gathering(stage, pipe):
            copy.start()
        whole[stage, pipe, :, pl.ds(me, 1)] = value.reshape(OWNED, 1, TILE, HALF)
        all_of(parts.at[pipe], rs_send.at[pipe])

    def gathered(stage, pipe):
        all_of(whole.at[stage, pipe, :, pl.ds(0, NPEERS)], ag_recv.at[pipe])
        all_of(parts.at[pipe], ag_send.at[pipe])

    def from_tiles(tiles):
        flat = tiles.reshape(TILES, TILE, HALF)
        left = flat[: TILES // 2].reshape(HEIGHT, HALF)
        right = flat[TILES // 2 :].reshape(HEIGHT, HALF)
        return jnp.concatenate([left, right], axis=1)

    def to_tiles(value):
        left = value[:, :HALF].reshape(TILES // 2, TILE, HALF)
        right = value[:, HALF:].reshape(TILES // 2, TILE, HALF)
        return jnp.concatenate([left, right], axis=0).reshape(OWNED, CHIPS, TILE, HALF)

    def weights(stage, pipe):
        high, low = split(from_tiles(whole[stage, pipe]))
        lhs_ab[0 : 2 * UNITS] = high[: 2 * UNITS]
        lhs_ab[2 * UNITS :] = low[: 2 * UNITS]
        lhs_c[0:UNITS] = high[2 * UNITS :]
        lhs_c[UNITS:] = low[2 * UNITS :]

    def projected(first, second, cols):
        pg = dot(lhs_ab[...], tok_t[first, :, cols])
        pg = pg[: 2 * UNITS] + pg[2 * UNITS :]
        uu = dot(lhs_c[...], tok_t[second, :, cols])
        return pg[:UNITS], pg[UNITS:], uu[:UNITS] + uu[UNITS:]

    def keep(cols, dp, dg, e, pipe):
        for i, value in enumerate((dp, dg)):
            high, low = split(value)
            d_pair[i * UNITS : (i + 1) * UNITS, cols] = high
            d_pair[(2 + i) * UNITS : (3 + i) * UNITS, cols] = low
        high, low = split(e)
        e_pair[pipe, 0:UNITS, cols] = high
        e_pair[pipe, UNITS:, cols] = low

    def contract(first, second, pipe):
        ab = dot(d_pair[...], tok_b[first])
        cc = dot(e_pair[pipe], tok_b[second])
        return jnp.concatenate(
            [ab[: 2 * UNITS] + ab[2 * UNITS :], cc[:UNITS] + cc[UNITS:]], axis=0
        )

    def scatter(pipe, value):
        part[pipe] = to_tiles(value)
        for copy in scattering(pipe):
            copy.start()

    def token_loop(body):
        for i in range(BOTH // COLS):
            body(slice(i * COLS, (i + 1) * COLS))

    def sigmoid(g):
        return 1.0 / (1.0 + jnp.exp(-g))

    def rates(cols):
        return jnp.concatenate([eta[:, cols]] * (UNITS // TILE), axis=0)

    def inner(stage, pipe):
        weights(stage, pipe)

        def body(cols):
            p, g, u = projected(0, 1, cols)
            s = sigmoid(g)
            act = g * s
            slope = s + act * (1.0 - s)
            rate = rates(cols)
            f1 = rate * act
            f3 = rate * p * slope
            pre_p[pipe, :, cols] = p
            pre_g[pipe, :, cols] = g
            pre_u[pipe, :, cols] = u
            c1[stage, pipe, :, cols] = f1
            c3[stage, pipe, :, cols] = f3
            keep(cols, f1 * u, f3 * u, f1 * p, pipe)

        token_loop(body)
        return contract(0, 1, pipe)

    def inner_second(stage, pipe):
        def body(cols):
            p, g, u = pre_p[pipe, :, cols], pre_g[pipe, :, cols], pre_u[pipe, :, cols]
            s = sigmoid(g)
            slope = s + g * s * (1.0 - s)
            bend = s * (1.0 - s) * (2.0 + g * (1.0 - 2.0 * s))
            w = rates(cols) * u
            c2[stage, pipe, :, cols] = w * slope
            c4[stage, pipe, :, cols] = w * p * bend

        token_loop(body)

    def outer(pipe):
        weights(2, pipe)

        def body(cols):
            p, g, u = projected(2, 3, cols)
            s = sigmoid(g)
            act = g * s
            slope = s + act * (1.0 - s)
            keep(cols, u * act, u * p * slope, act * p, pipe)

        token_loop(body)
        return contract(2, 3, pipe)

    def hessian(stage, direction, pipe):
        weights(direction, pipe)

        def body(cols):
            p, g, u = projected(0, 1, cols)
            f1, f2 = c1[stage, pipe, :, cols], c2[stage, pipe, :, cols]
            f3, f4 = c3[stage, pipe, :, cols], c4[stage, pipe, :, cols]
            keep(cols, f1 * u + f2 * g, f3 * u + f2 * p + f4 * g, f3 * g + f1 * p, pipe)

        token_loop(body)
        return contract(0, 1, pipe)

    all_of(natural.at[:, pl.ds(0, NPEERS)], n_recv)
    all_of(natural.at[:, pl.ds(0, NPEERS)], n_send)
    flipped = [
        natural[2 * i : 2 * i + 2].reshape(WIDTH, HALF).T for i in range(3)
    ]
    for pipe in range(PIPES):
        rows = slice(pipe * UNITS, (pipe + 1) * UNITS)
        whole[0, pipe] = to_tiles(jnp.concatenate([matrix[rows] for matrix in flipped], axis=0))

    def mine_of(stage, pipe):
        return whole[stage, pipe, :, pl.ds(me, 1)].reshape(OWNED, TILE, HALF)

    for pipe in range(PIPES):
        scatter(pipe, inner(0, pipe))
    for pipe in range(PIPES):
        inner_second(0, pipe)
    for pipe in range(PIPES):
        gather(1, pipe, mine_of(0, pipe) - reduced(pipe))
    for pipe in range(PIPES):
        gathered(1, pipe)
        scatter(pipe, inner(1, pipe))
    for pipe in range(PIPES):
        inner_second(1, pipe)
    for pipe in range(PIPES):
        gather(2, pipe, mine_of(1, pipe) - reduced(pipe))

    for pipe in range(PIPES):
        gathered(2, pipe)
        scatter(pipe, outer(pipe))

    def partial_out(cols):
        total = None
        for pipe in range(PIPES):
            ct_high, ct_low = split(from_tiles(whole[2, pipe])[2 * UNITS :])
            high = e_pair[pipe, 0:UNITS, cols].astype(F32).T.astype(BF16)
            low = e_pair[pipe, UNITS:, cols].astype(F32).T.astype(BF16)
            term = dot(high, ct_high) + (dot(high, ct_low) + dot(low, ct_high))
            total = term if total is None else total + term
        return total

    out_part[...] = partial_out(slice(TOKENS, BOTH))
    swap = pltpu.make_async_remote_copy(
        out_part, out_other, o_send, o_recv, device_id=other, device_id_type=MESH
    )
    swap.start()
    out_own[...] = partial_out(slice(0, TOKENS))
    for pipe in range(PIPES):
        gather(3, pipe, reduced(pipe))
    swap.wait()
    out_ref[0] = (out_own[...] + out_other[...]).astype(BF16)

    for pipe in range(PIPES):
        gathered(3, pipe)
        scatter(pipe, hessian(1, 3, pipe))
    for pipe in range(PIPES):
        gather(4, pipe, mine_of(3, pipe) - reduced(pipe))

    first_half = lax.broadcasted_iota(jnp.int32, (LAYERS, STRIP, HALF), 2) < UNITS

    def upright(value):
        turned = []
        for i in range(3):
            matrix = value[i * UNITS : (i + 1) * UNITS]
            turned.append(jnp.concatenate([matrix, matrix], axis=0).T)
        blocks = jnp.concatenate(turned, axis=0).reshape(LAYERS, 2, STRIP, HALF)
        packed = jnp.where(first_half, blocks[:, 0], blocks[:, 1])
        return packed.reshape(OWNED, CHIPS, TILE, HALF)

    for pipe in range(PIPES):
        gathered(4, pipe)
        part[pipe] = upright(hessian(0, 4, pipe))
        for copy in scattering(pipe):
            copy.start()

    last_sub = lax.rem(me + SHARE * LAYERS - SHARE * z, CHIPS)
    last_at = lax.div(SHARE * z + last_sub, CHIPS)
    last_owner = last_sub < SHARE

    def to_owner(pipe, j):
        target = lax.div(CHIPS * j + me, SHARE)
        slot = lax.rem(target + LAYERS - z, LAYERS)
        return target, pltpu.make_async_remote_copy(
            chunk.at[pipe, j], z_parts.at[pipe, slot - 1], y_send.at[pipe, j], y_recv.at[pipe],
            device_id=(x, y, c, target), device_id_type=MESH,
        )

    for pipe in range(PIPES):
        adj[pipe] = upright(from_tiles(whole[4, pipe]))
    for pipe in range(PIPES):
        chunk[pipe] = adj[pipe, :, pl.ds(me, 1)].reshape(OWNED, TILE, HALF) - reduced(pipe)
        for j in range(OWNED):
            target, copy = to_owner(pipe, j)

            @pl.when(target != z)
            def _():
                copy.start()

        all_of(parts.at[pipe], rs_send.at[pipe])

    def spread():
        return [
            pltpu.make_async_remote_copy(
                z_sum, tail.at[c, last_sub], t_send, t_recv.at[c, last_sub],
                device_id=device, device_id_type=MESH,
            )
            for device in everyone
        ]

    @pl.when(last_owner)
    def _():
        for pipe in range(PIPES):
            all_of(z_parts.at[pipe], y_recv.at[pipe])
            total = chunk[pipe, pl.ds(last_at, 1)].reshape(TILE, HALF)
            for slot in range(LAYERS - 1):
                total = total + z_parts[pipe, slot]
            z_sum[pipe] = total
        for copy in spread():
            copy.start()
        tail[pl.ds(c, 1), pl.ds(last_sub, 1)] = z_sum[...].reshape(1, 1, PIPES, TILE, HALF)

    for pipe in range(PIPES):
        for j in range(OWNED):
            target, copy = to_owner(pipe, j)

            @pl.when(target != z)
            def _():
                copy.wait_send()

    for s in range(SHARE):
        source = lax.rem(SHARE * z + s, CHIPS)
        for core in range(2):

            @pl.when((source != me) | (c != core))
            def _():
                pltpu.make_async_remote_copy(
                    z_sum, tail.at[core, s], t_send, t_recv.at[core, s],
                    device_id=other, device_id_type=MESH,
                ).wait_recv()

    low = lax.broadcasted_iota(jnp.int32, (TILE, HALF), 1) < UNITS
    for core in range(2):
        for s in range(SHARE):
            one, two = tail[core, s, 0], tail[core, s, 1]
            cols = slice(core * HALF, (core + 1) * HALF)
            grad_ref[s, :, cols] = jnp.where(low, one, pltpu.roll(two, UNITS, 1))
            grad_ref[SHARE + s, :, cols] = jnp.where(low, pltpu.roll(one, UNITS, 1), two)

    @pl.when(last_owner)
    def _():
        all_of(waits, t_send)


def body(queries, key_rows, value_rows, step_rates, cotangent, fast_init):
    vmem = lambda *shape: pltpu.VMEM(shape, F32)
    half = lambda *shape: pltpu.VMEM(shape, BF16)
    dma = lambda *shape: pltpu.SemaphoreType.DMA(shape)
    vmem_spec = pl.BlockSpec(memory_space=pltpu.VMEM)
    any_spec = pl.BlockSpec(memory_space=pl.ANY)
    result, grad = pl.pallas_call(
        kernel,
        out_shape=(
            pltpu.VMEM(queries.shape, BF16),
            pltpu.VMEM((GROUPS, TILE, WIDTH), F32),
        ),
        in_specs=[any_spec] * 6,
        out_specs=(vmem_spec, vmem_spec),
        scratch_shapes=[
            half(4, TOKENS, WIDTH),
            vmem(4, TOKENS, WIDTH),
            vmem(4, TOKENS, WIDTH),
            half(4, BOTH, WIDTH),
            half(4, WIDTH, BOTH),
            vmem(1, TOKENS),
            vmem(1, TOKENS),
            vmem(TILE, BOTH),
            vmem(GROUPS, TILE, HALF),
            vmem(GROUPS, CHIPS, TILE, HALF),
            vmem(GROUPS, TILE, HALF),
            vmem(PIPES, OWNED, CHIPS, TILE, HALF),
            vmem(5, PIPES, OWNED, CHIPS, TILE, HALF),
            vmem(PIPES, OWNED, CHIPS, TILE, HALF),
            vmem(PIPES, NPEERS, OWNED, TILE, HALF),
            vmem(PIPES, OWNED, TILE, HALF),
            half(4 * UNITS, WIDTH),
            half(2 * UNITS, WIDTH),
            vmem(PIPES, UNITS, BOTH),
            vmem(PIPES, UNITS, BOTH),
            vmem(PIPES, UNITS, BOTH),
            vmem(2, PIPES, UNITS, BOTH),
            vmem(2, PIPES, UNITS, BOTH),
            vmem(2, PIPES, UNITS, BOTH),
            vmem(2, PIPES, UNITS, BOTH),
            half(4 * UNITS, BOTH),
            half(PIPES, 2 * UNITS, BOTH),
            vmem(TOKENS, WIDTH),
            vmem(TOKENS, WIDTH),
            vmem(TOKENS, WIDTH),
            vmem(PIPES, LAYERS - 1, TILE, HALF),
            vmem(PIPES, TILE, HALF),
            vmem(2, SHARE, PIPES, TILE, HALF),
            vmem(2 * NPEERS + 1, PIPES, TILE, HALF),
            dma(6),
            dma(4), dma(4),
            pltpu.SemaphoreType.DMA, pltpu.SemaphoreType.DMA,
            pltpu.SemaphoreType.DMA, pltpu.SemaphoreType.DMA,
            pltpu.SemaphoreType.DMA, pltpu.SemaphoreType.DMA,
            dma(PIPES), dma(PIPES),
            dma(PIPES), dma(PIPES),
            dma(len(Z_STEPS)), dma(GROUPS), dma(GROUPS),
            dma(PIPES, OWNED), dma(PIPES),
            pltpu.SemaphoreType.DMA, dma(2, SHARE),
        ],
        compiler_params=pltpu.CompilerParams(
            collective_id=0, has_side_effects=True, vmem_limit_bytes=56 * 2**20
        ),
    )(queries, key_rows, value_rows, step_rates, cotangent, fast_init.reshape(GROUPS, TILE, WIDTH))
    return result, grad.reshape(fast_init.shape)


def solution(mesh):
    torus = Mesh(
        mesh.devices.reshape(SIDE, SIDE, 2, mesh.shape["batch"]), ("x", "y", "c", "z")
    )
    return jax.shard_map(
        body,
        mesh=torus,
        in_specs=(
            P("z", SEQ, None),
            P("z", SEQ, None),
            P("z", SEQ, None),
            P("z", SEQ),
            P("z", SEQ, None),
            P("z", None),
        ),
        out_specs=(P("z", SEQ, None), P("z", None)),
        check_vma=False,
    )
```

```python
import math

import jax
import jax.numpy as jnp
from jax import lax
from jax.experimental import pallas as pl
from jax.experimental.pallas import tpu as pltpu
from jax.sharding import Mesh
from jax.sharding import PartitionSpec as P

MESH = pl.DeviceIdType.MESH
SEQ = ("x", "y", "c")
F32 = jnp.float32
BF16 = jnp.bfloat16
SIDE = 4
CHIPS = SIDE * SIDE
LAYERS = 16
TILE = 8
TOKENS = 512
WIDTH = 256
HALF = 128
GROUPS = 6
COLS = 256
BOTH = 2 * TOKENS
PIPES = 2
UNITS = HALF // PIPES
HEIGHT = 3 * UNITS
TILES = 2 * HEIGHT // TILE
OWNED = TILES // CHIPS
STRIP = GROUPS * TILE // PIPES
SHARE = STRIP // TILE
NEAR = 4


def far_first():
    hops = lambda step: min(step, SIDE - step)
    steps = [(dx, dy) for dx in range(SIDE) for dy in range(SIDE) if dx or dy]
    return sorted(steps, key=lambda s: -(hops(s[0]) + hops(s[1])))


PEERS = far_first()
NPEERS = len(PEERS)
Z_STEPS = [d for dz in range(NEAR, 0, -1) for d in (dz, LAYERS - dz)]


def split(value):
    high = value.astype(BF16)
    return high, (value - high.astype(F32)).astype(BF16)


def dot(a, b):
    return jnp.dot(a, b, preferred_element_type=F32)


def kernel(
    q_in, k_in, v_in, rates_in, cot_in, w_in,
    out_ref, grad_ref,
    tok, mine, theirs, tok_b, tok_t, rates_own, rates_other, eta, w_own,
    natural, n_chunk, adj,
    whole, part, parts, chunk,
    lhs_ab, lhs_c,
    pre_p, pre_g, pre_u, c1, c2, c3, c4,
    d_pair, e_pair, out_own, out_part, out_other, z_parts, z_sum, tail, waits,
    load_sem, x_send, x_recv, r_send, r_recv, o_send, o_recv,
    n_send, n_recv, rs_send, rs_recv, ag_send, ag_recv,
    z_send, z_recv, zz_send, y_send, y_recv, t_send, t_recv,
):
    x, y, c, z = (lax.axis_index(name) for name in ("x", "y", "c", "z"))
    me = x * SIDE + y
    other = (x, y, 1 - c, z)

    def peer(step):
        px = lax.rem(x + step[0], SIDE)
        py = lax.rem(y + step[1], SIDE)
        return (px, py, c, z), px * SIDE + py

    def z_peer(dz):
        return (x, y, c, lax.rem(z + dz, LAYERS))

    peers = [peer(step) for step in PEERS]
    everyone = [(d[0], d[1], core, z) for d, _ in peers for core in (c, 1 - c)] + [other]

    barrier = pltpu.get_barrier_semaphore()
    greeted = [z_peer(dz) for dz in Z_STEPS] + everyone
    for device in greeted:
        pl.semaphore_signal(barrier, inc=1, device_id=device, device_id_type=MESH)

    loads = [
        pltpu.make_async_copy(src.at[0], tok.at[i], load_sem.at[i])
        for i, src in enumerate((k_in, v_in, q_in, cot_in))
    ]
    loads.append(pltpu.make_async_copy(rates_in, rates_own, load_sem.at[4]))
    for half in range(2):
        @pl.when(c == half)
        def _():
            pltpu.make_async_copy(
                w_in.at[:, :, half * HALF : (half + 1) * HALF], w_own, load_sem.at[5]
            ).start()
    for load in loads:
        load.start()

    divisor = math.sqrt(lax.axis_size(SEQ) * TOKENS)
    for load in loads:
        load.wait()
    for i in range(4):
        mine[i] = tok[i].astype(F32)
    eta[:, 0:TOKENS] = jnp.broadcast_to(-(rates_own[...] / divisor), (TILE, TOKENS))

    pltpu.make_async_copy(w_own, w_own, load_sem.at[5]).wait()
    pl.semaphore_wait(barrier, len(greeted))

    sub = lax.rem(me + GROUPS * LAYERS - GROUPS * z, CHIPS)
    group = GROUPS * z + sub
    at = lax.div(group, CHIPS)
    owner = sub < GROUPS

    def z_copy(i):
        return pltpu.make_async_remote_copy(
            w_own.at[sub], n_chunk.at[at], z_send.at[i], z_recv.at[at],
            device_id=z_peer(Z_STEPS[i]), device_id_type=MESH,
        )

    @pl.when(owner)
    def _():
        for i in range(len(Z_STEPS)):
            z_copy(i).start()
        n_chunk[pl.ds(at, 1)] = w_own[pl.ds(sub, 1)]

    swaps = [
        pltpu.make_async_remote_copy(
            mine.at[i], theirs.at[i], x_send.at[i], x_recv.at[i], device_id=other, device_id_type=MESH
        )
        for i in range(4)
    ]
    swaps.append(
        pltpu.make_async_remote_copy(
            rates_own, rates_other, r_send, r_recv, device_id=other, device_id_type=MESH
        )
    )
    for swap in swaps:
        swap.start()

    def own_tokens(i):
        tok_b[i, 0:TOKENS] = tok[i]
        tok_t[i, :, 0:TOKENS] = mine[i].T.astype(BF16)

    def other_tokens(i):
        swaps[i].wait()
        tok_b[i, TOKENS:BOTH] = theirs[i].astype(BF16)
        tok_t[i, :, TOKENS:BOTH] = theirs[i].T.astype(BF16)

    for i in range(2):
        own_tokens(i)

    def z_pass(j, steps):
        dz = NEAR if steps > 0 else LAYERS - NEAR
        return pltpu.make_async_remote_copy(
            n_chunk.at[j], n_chunk.at[j], zz_send.at[j], z_recv.at[j],
            device_id=z_peer(dz), device_id_type=MESH,
        )

    def z_away(j):
        return lax.rem(z + LAYERS - lax.div(CHIPS * j + me, GROUPS), LAYERS)

    def z_landed(j):
        pltpu.make_async_remote_copy(
            w_own.at[0], n_chunk.at[j], z_send.at[0], z_recv.at[j], device_id=other, device_id_type=MESH
        ).wait_recv()

    def up(j):
        return (z_away(j) >= 1) & (z_away(j) <= NEAR)

    def down(j):
        return z_away(j) >= LAYERS - NEAR + 1

    for j in range(GROUPS):
        @pl.when(up(j))
        def _():
            z_landed(j)
            z_pass(j, 1).start()

        @pl.when(down(j))
        def _():
            z_landed(j)
            z_pass(j, -1).start()

        @pl.when(z_away(j) == LAYERS - NEAR)
        def _():
            z_landed(j)

    def pass_round(j):
        for device, _ in peers:
            pltpu.make_async_remote_copy(
                n_chunk.at[j], natural.at[j, me], n_send, n_recv, device_id=device, device_id_type=MESH
            ).start()
        natural[j, pl.ds(me, 1)] = n_chunk[pl.ds(j, 1)]

    def far(j):
        return (z_away(j) > NEAR) & (z_away(j) < LAYERS - NEAR)

    for j in range(GROUPS):
        @pl.when((z_away(j) <= NEAR) | (z_away(j) >= LAYERS - NEAR))
        def _():
            pass_round(j)

    for i in range(2):
        other_tokens(i)
    swaps[4].wait()
    eta[:, TOKENS:BOTH] = jnp.broadcast_to(-(rates_other[...] / divisor), (TILE, TOKENS))

    for j in range(GROUPS):
        @pl.when(far(j))
        def _():
            z_landed(j)
            pass_round(j)

    for i in (2, 3):
        own_tokens(i)
        other_tokens(i)

    @pl.when(owner)
    def _():
        for i in range(len(Z_STEPS)):
            z_copy(i).wait_send()

    for j in range(GROUPS):
        @pl.when(up(j))
        def _():
            z_pass(j, 1).wait_send()

        @pl.when(down(j))
        def _():
            z_pass(j, -1).wait_send()

    def all_of(landed, semaphore):
        pltpu.make_async_copy(landed, landed, semaphore).wait()

    def gathering(stage, pipe):
        return [
            pltpu.make_async_remote_copy(
                chunk.at[pipe], whole.at[stage, pipe, :, me], ag_send.at[pipe], ag_recv.at[pipe],
                device_id=device, device_id_type=MESH,
            )
            for device, _ in peers
        ]

    def scattering(pipe):
        return [
            pltpu.make_async_remote_copy(
                part.at[pipe, :, chip], parts.at[pipe, k], rs_send.at[pipe], rs_recv.at[pipe],
                device_id=device, device_id_type=MESH,
            )
            for k, (device, chip) in enumerate(peers)
        ]

    def reduced(pipe):
        all_of(parts.at[pipe], rs_recv.at[pipe])
        total = part[pipe, :, pl.ds(me, 1)].reshape(OWNED, TILE, HALF)
        for k in range(NPEERS):
            total = total + parts[pipe, k]
        return total

    def gather(stage, pipe, value):
        chunk[pipe] = value
        for copy in gathering(stage, pipe):
            copy.start()
        whole[stage, pipe, :, pl.ds(me, 1)] = value.reshape(OWNED, 1, TILE, HALF)
        all_of(parts.at[pipe], rs_send.at[pipe])

    def gathered(stage, pipe):
        all_of(whole.at[stage, pipe, :, pl.ds(0, NPEERS)], ag_recv.at[pipe])
        all_of(parts.at[pipe], ag_send.at[pipe])

    def from_tiles(tiles):
        flat = tiles.reshape(TILES, TILE, HALF)
        left = flat[: TILES // 2].reshape(HEIGHT, HALF)
        right = flat[TILES // 2 :].reshape(HEIGHT, HALF)
        return jnp.concatenate([left, right], axis=1)

    def to_tiles(value):
        left = value[:, :HALF].reshape(TILES // 2, TILE, HALF)
        right = value[:, HALF:].reshape(TILES // 2, TILE, HALF)
        return jnp.concatenate([left, right], axis=0).reshape(OWNED, CHIPS, TILE, HALF)

    def weights(stage, pipe):
        high, low = split(from_tiles(whole[stage, pipe]))
        lhs_ab[0 : 2 * UNITS] = high[: 2 * UNITS]
        lhs_ab[2 * UNITS :] = low[: 2 * UNITS]
        lhs_c[0:UNITS] = high[2 * UNITS :]
        lhs_c[UNITS:] = low[2 * UNITS :]

    def projected(first, second, cols):
        pg = dot(lhs_ab[...], tok_t[first, :, cols])
        pg = pg[: 2 * UNITS] + pg[2 * UNITS :]
        uu = dot(lhs_c[...], tok_t[second, :, cols])
        return pg[:UNITS], pg[UNITS:], uu[:UNITS] + uu[UNITS:]

    def keep(cols, dp, dg, e, pipe):
        for i, value in enumerate((dp, dg)):
            high, low = split(value)
            d_pair[i * UNITS : (i + 1) * UNITS, cols] = high
            d_pair[(2 + i) * UNITS : (3 + i) * UNITS, cols] = low
        high, low = split(e)
        e_pair[pipe, 0:UNITS, cols] = high
        e_pair[pipe, UNITS:, cols] = low

    def contract(first, second, pipe):
        ab = dot(d_pair[...], tok_b[first])
        cc = dot(e_pair[pipe], tok_b[second])
        return jnp.concatenate(
            [ab[: 2 * UNITS] + ab[2 * UNITS :], cc[:UNITS] + cc[UNITS:]], axis=0
        )

    def scatter(pipe, value):
        part[pipe] = to_tiles(value)
        for copy in scattering(pipe):
            copy.start()

    def token_loop(body):
        for i in range(BOTH // COLS):
            body(slice(i * COLS, (i + 1) * COLS))

    def sigmoid(g):
        return 1.0 / (1.0 + jnp.exp(-g))

    def rates(cols):
        return jnp.concatenate([eta[:, cols]] * (UNITS // TILE), axis=0)

    def inner(stage, pipe):
        weights(stage, pipe)

        def body(cols):
            p, g, u = projected(0, 1, cols)
            s = sigmoid(g)
            act = g * s
            slope = s + act * (1.0 - s)
            rate = rates(cols)
            f1 = rate * act
            f3 = rate * p * slope
            pre_p[pipe, :, cols] = p
            pre_g[pipe, :, cols] = g
            pre_u[pipe, :, cols] = u
            c1[stage, pipe, :, cols] = f1
            c3[stage, pipe, :, cols] = f3
            keep(cols, f1 * u, f3 * u, f1 * p, pipe)

        token_loop(body)
        return contract(0, 1, pipe)

    def inner_second(stage, pipe):
        def body(cols):
            p, g, u = pre_p[pipe, :, cols], pre_g[pipe, :, cols], pre_u[pipe, :, cols]
            s = sigmoid(g)
            slope = s + g * s * (1.0 - s)
            bend = s * (1.0 - s) * (2.0 + g * (1.0 - 2.0 * s))
            w = rates(cols) * u
            c2[stage, pipe, :, cols] = w * slope
            c4[stage, pipe, :, cols] = w * p * bend

        token_loop(body)

    def outer(pipe):
        weights(2, pipe)

        def body(cols):
            p, g, u = projected(2, 3, cols)
            s = sigmoid(g)
            act = g * s
            slope = s + act * (1.0 - s)
            keep(cols, u * act, u * p * slope, act * p, pipe)

        token_loop(body)
        return contract(2, 3, pipe)

    def hessian(stage, direction, pipe):
        weights(direction, pipe)

        def body(cols):
            p, g, u = projected(0, 1, cols)
            f1, f2 = c1[stage, pipe, :, cols], c2[stage, pipe, :, cols]
            f3, f4 = c3[stage, pipe, :, cols], c4[stage, pipe, :, cols]
            keep(cols, f1 * u + f2 * g, f3 * u + f2 * p + f4 * g, f3 * g + f1 * p, pipe)

        token_loop(body)
        return contract(0, 1, pipe)

    all_of(natural.at[:, pl.ds(0, NPEERS)], n_recv)
    all_of(natural.at[:, pl.ds(0, NPEERS)], n_send)
    flipped = [
        natural[2 * i : 2 * i + 2].reshape(WIDTH, HALF).T for i in range(3)
    ]
    for pipe in range(PIPES):
        rows = slice(pipe * UNITS, (pipe + 1) * UNITS)
        whole[0, pipe] = to_tiles(jnp.concatenate([matrix[rows] for matrix in flipped], axis=0))
        scatter(pipe, inner(0, pipe))

    def mine_of(stage, pipe):
        return whole[stage, pipe, :, pl.ds(me, 1)].reshape(OWNED, TILE, HALF)

    for pipe in range(PIPES):
        inner_second(0, pipe)
    for pipe in range(PIPES):
        gather(1, pipe, mine_of(0, pipe) - reduced(pipe))
    for pipe in range(PIPES):
        gathered(1, pipe)
        scatter(pipe, inner(1, pipe))
    for pipe in range(PIPES):
        inner_second(1, pipe)
    for pipe in range(PIPES):
        gather(2, pipe, mine_of(1, pipe) - reduced(pipe))

    for pipe in range(PIPES):
        gathered(2, pipe)
        scatter(pipe, outer(pipe))

    def partial_out(cols):
        total = None
        for pipe in range(PIPES):
            ct_high, ct_low = split(from_tiles(whole[2, pipe])[2 * UNITS :])
            high = e_pair[pipe, 0:UNITS, cols].astype(F32).T.astype(BF16)
            low = e_pair[pipe, UNITS:, cols].astype(F32).T.astype(BF16)
            term = dot(high, ct_high) + (dot(high, ct_low) + dot(low, ct_high))
            total = term if total is None else total + term
        return total

    out_part[...] = partial_out(slice(TOKENS, BOTH))
    swap = pltpu.make_async_remote_copy(
        out_part, out_other, o_send, o_recv, device_id=other, device_id_type=MESH
    )
    swap.start()
    out_own[...] = partial_out(slice(0, TOKENS))
    for pipe in range(PIPES):
        gather(3, pipe, reduced(pipe))
    swap.wait()
    out_ref[0] = (out_own[...] + out_other[...]).astype(BF16)

    for pipe in range(PIPES):
        gathered(3, pipe)
        scatter(pipe, hessian(1, 3, pipe))
    for pipe in range(PIPES):
        gather(4, pipe, mine_of(3, pipe) - reduced(pipe))

    first_half = lax.broadcasted_iota(jnp.int32, (LAYERS, STRIP, HALF), 2) < UNITS

    def upright(value):
        turned = []
        for i in range(3):
            matrix = value[i * UNITS : (i + 1) * UNITS]
            turned.append(jnp.concatenate([matrix, matrix], axis=0).T)
        blocks = jnp.concatenate(turned, axis=0).reshape(LAYERS, 2, STRIP, HALF)
        packed = jnp.where(first_half, blocks[:, 0], blocks[:, 1])
        return packed.reshape(OWNED, CHIPS, TILE, HALF)

    for pipe in range(PIPES):
        gathered(4, pipe)
        part[pipe] = upright(hessian(0, 4, pipe))
        for copy in scattering(pipe):
            copy.start()

    last_sub = lax.rem(me + SHARE * LAYERS - SHARE * z, CHIPS)
    last_at = lax.div(SHARE * z + last_sub, CHIPS)
    last_owner = last_sub < SHARE

    def to_owner(pipe, j):
        target = lax.div(CHIPS * j + me, SHARE)
        slot = lax.rem(target + LAYERS - z, LAYERS)
        return target, pltpu.make_async_remote_copy(
            chunk.at[pipe, j], z_parts.at[pipe, slot - 1], y_send.at[pipe, j], y_recv.at[pipe],
            device_id=(x, y, c, target), device_id_type=MESH,
        )

    for pipe in range(PIPES):
        adj[pipe] = upright(from_tiles(whole[4, pipe]))
    for pipe in range(PIPES):
        chunk[pipe] = adj[pipe, :, pl.ds(me, 1)].reshape(OWNED, TILE, HALF) - reduced(pipe)
        for j in range(OWNED):
            target, copy = to_owner(pipe, j)

            @pl.when(target != z)
            def _():
                copy.start()

        all_of(parts.at[pipe], rs_send.at[pipe])

    def spread():
        return [
            pltpu.make_async_remote_copy(
                z_sum, tail.at[c, last_sub], t_send, t_recv.at[c, last_sub],
                device_id=device, device_id_type=MESH,
            )
            for device in everyone
        ]

    @pl.when(last_owner)
    def _():
        for pipe in range(PIPES):
            all_of(z_parts.at[pipe], y_recv.at[pipe])
            total = chunk[pipe, pl.ds(last_at, 1)].reshape(TILE, HALF)
            for slot in range(LAYERS - 1):
                total = total + z_parts[pipe, slot]
            z_sum[pipe] = total
        for copy in spread():
            copy.start()
        tail[pl.ds(c, 1), pl.ds(last_sub, 1)] = z_sum[...].reshape(1, 1, PIPES, TILE, HALF)

    for pipe in range(PIPES):
        for j in range(OWNED):
            target, copy = to_owner(pipe, j)

            @pl.when(target != z)
            def _():
                copy.wait_send()

    for s in range(SHARE):
        source = lax.rem(SHARE * z + s, CHIPS)
        for core in range(2):

            @pl.when((source != me) | (c != core))
            def _():
                pltpu.make_async_remote_copy(
                    z_sum, tail.at[core, s], t_send, t_recv.at[core, s],
                    device_id=other, device_id_type=MESH,
                ).wait_recv()

    low = lax.broadcasted_iota(jnp.int32, (TILE, HALF), 1) < UNITS
    for core in range(2):
        for s in range(SHARE):
            one, two = tail[core, s, 0], tail[core, s, 1]
            cols = slice(core * HALF, (core + 1) * HALF)
            grad_ref[s, :, cols] = jnp.where(low, one, pltpu.roll(two, UNITS, 1))
            grad_ref[SHARE + s, :, cols] = jnp.where(low, pltpu.roll(one, UNITS, 1), two)

    @pl.when(last_owner)
    def _():
        all_of(waits, t_send)


def hand_over(out_in, grad_in, out_ref, grad_ref, sems):
    copies = [
        pltpu.make_async_copy(grad_in, grad_ref, sems.at[0]),
        pltpu.make_async_copy(out_in, out_ref, sems.at[1]),
    ]
    for copy in copies:
        copy.start()
    for copy in copies:
        copy.wait()


def body(queries, key_rows, value_rows, step_rates, cotangent, fast_init):
    vmem = lambda *shape: pltpu.VMEM(shape, F32)
    half = lambda *shape: pltpu.VMEM(shape, BF16)
    dma = lambda *shape: pltpu.SemaphoreType.DMA(shape)
    vmem_spec = pl.BlockSpec(memory_space=pltpu.VMEM)
    any_spec = pl.BlockSpec(memory_space=pl.ANY)
    result, grad = pl.pallas_call(
        kernel,
        out_shape=(
            pltpu.VMEM(queries.shape, BF16),
            pltpu.VMEM((GROUPS, TILE, WIDTH), F32),
        ),
        in_specs=[any_spec] * 6,
        out_specs=(vmem_spec, vmem_spec),
        scratch_shapes=[
            half(4, TOKENS, WIDTH),
            vmem(4, TOKENS, WIDTH),
            vmem(4, TOKENS, WIDTH),
            half(4, BOTH, WIDTH),
            half(4, WIDTH, BOTH),
            vmem(1, TOKENS),
            vmem(1, TOKENS),
            vmem(TILE, BOTH),
            vmem(GROUPS, TILE, HALF),
            vmem(GROUPS, CHIPS, TILE, HALF),
            vmem(GROUPS, TILE, HALF),
            vmem(PIPES, OWNED, CHIPS, TILE, HALF),
            vmem(5, PIPES, OWNED, CHIPS, TILE, HALF),
            vmem(PIPES, OWNED, CHIPS, TILE, HALF),
            vmem(PIPES, NPEERS, OWNED, TILE, HALF),
            vmem(PIPES, OWNED, TILE, HALF),
            half(4 * UNITS, WIDTH),
            half(2 * UNITS, WIDTH),
            vmem(PIPES, UNITS, BOTH),
            vmem(PIPES, UNITS, BOTH),
            vmem(PIPES, UNITS, BOTH),
            vmem(2, PIPES, UNITS, BOTH),
            vmem(2, PIPES, UNITS, BOTH),
            vmem(2, PIPES, UNITS, BOTH),
            vmem(2, PIPES, UNITS, BOTH),
            half(4 * UNITS, BOTH),
            half(PIPES, 2 * UNITS, BOTH),
            vmem(TOKENS, WIDTH),
            vmem(TOKENS, WIDTH),
            vmem(TOKENS, WIDTH),
            vmem(PIPES, LAYERS - 1, TILE, HALF),
            vmem(PIPES, TILE, HALF),
            vmem(2, SHARE, PIPES, TILE, HALF),
            vmem(2 * NPEERS + 1, PIPES, TILE, HALF),
            dma(6),
            dma(4), dma(4),
            pltpu.SemaphoreType.DMA, pltpu.SemaphoreType.DMA,
            pltpu.SemaphoreType.DMA, pltpu.SemaphoreType.DMA,
            pltpu.SemaphoreType.DMA, pltpu.SemaphoreType.DMA,
            dma(PIPES), dma(PIPES),
            dma(PIPES), dma(PIPES),
            dma(len(Z_STEPS)), dma(GROUPS), dma(GROUPS),
            dma(PIPES, OWNED), dma(PIPES),
            pltpu.SemaphoreType.DMA, dma(2, SHARE),
        ],
        compiler_params=pltpu.CompilerParams(
            collective_id=0, has_side_effects=True, vmem_limit_bytes=56 * 2**20
        ),
    )(queries, key_rows, value_rows, step_rates, cotangent, fast_init.reshape(GROUPS, TILE, WIDTH))
    result = pltpu.with_memory_space_constraint(result, pltpu.VMEM)
    grad = pltpu.with_memory_space_constraint(grad, pltpu.VMEM)
    result, grad = pl.pallas_call(
        hand_over,
        out_shape=(
            jax.ShapeDtypeStruct(queries.shape, BF16),
            jax.ShapeDtypeStruct((GROUPS, TILE, WIDTH), F32),
        ),
        in_specs=[vmem_spec] * 2,
        out_specs=(any_spec,) * 2,
        scratch_shapes=[dma(2)],
    )(result, grad)
    return result, grad.reshape(fast_init.shape)


def solution(mesh):
    torus = Mesh(
        mesh.devices.reshape(SIDE, SIDE, 2, mesh.shape["batch"]), ("x", "y", "c", "z")
    )
    return jax.shard_map(
        body,
        mesh=torus,
        in_specs=(
            P("z", SEQ, None),
            P("z", SEQ, None),
            P("z", SEQ, None),
            P("z", SEQ),
            P("z", SEQ, None),
            P("z", None),
        ),
        out_specs=(P("z", SEQ, None), P("z", None)),
        check_vma=False,
    )
```
